256 devices in a mesh: inst: 16 (over x, y), section: 8 (over z), tp: 2 (over core).
Axes of the slice: x: 4, y: 4, z: 8, core: 2. Of those that a mesh axis runs over, the one named last changes fastest.
Arguments:
- tokens: bfloat16 [16, 1024, 8192], P('inst', None, 'section'), may hold values from -40 to 40
- norm_gain: float32 [8192], P('section'), may hold values from 0.4 to 6
- query_weight: bfloat16 [8192, 4096], P(('section', 'inst'), 'tp'), may hold values from -1 to 1
- key_weight: bfloat16 [8192, 1024], P(('section', 'inst'), 'tp'), may hold values from -1 to 1
- value_matrix: bfloat16 [8192, 1024], P(('section', 'inst'), 'tp'), may hold values from -0.0625 to 0.0625
Outputs:
- attended: bfloat16 [16, 1024, 4096], P('inst', 'section', 'tp')
- rotated_key_cache: bfloat16 [16, 1024, 1024], P('inst', 'section', 'tp')
- value_store_cache: bfloat16 [16, 1024, 1024], P('inst', 'section', 'tp')
The draws below stay inside these ranges and needn't reach their ends.
All inputs are finite; a program needn't handle non-finite values.
Results may differ from the reference program's by a relative error of at most 0.04.
Values may be sent and summed in bfloat16 or wider, within the bound.
No kernel may reach another device: no remote copies, remote signals or barrier semaphores. Data moves between devices by JAX's collectives and lax.ppermute only.
A program may use at most 64 MiB of HBM per device.

```python
import jax
import jax.numpy as jnp
from jax import lax

MODEL_WIDTH = 8192
QUERY_HEAD_SLICE = 32
KEY_VALUE_HEADS = 8
HEAD_SIZE = 128
PROMPT_LENGTH = 1024
INSTS = 16


def shared_keys(key):
    base_offset = jax.random.fold_in(key, 101)
    value_rows = jnp.clip(jax.random.normal(base_offset, (MODEL_WIDTH, KEY_VALUE_HEADS * HEAD_SIZE), jnp.float32), -6.0, 6.0)
    return value_rows / jnp.sqrt(jnp.float32(MODEL_WIDTH))


def draw_tokens(key, part):
    key = jax.random.fold_in(key, 11)
    noise_key, row_key = jax.random.split(key, 2)
    rows = jnp.exp(jax.random.uniform(row_key, (INSTS, PROMPT_LENGTH, 1), jnp.float32, 0.0, 1.0986))
    ramp = 0.6 + 1.2 * jnp.arange(MODEL_WIDTH).astype(jnp.float32) / MODEL_WIDTH
    noise = jnp.clip(jax.random.normal(noise_key, (INSTS, PROMPT_LENGTH, MODEL_WIDTH), jnp.float32), -6.0, 6.0)
    value_rows = noise * rows * ramp
    return jnp.clip(value_rows, -40.0, 40.0).astype(jnp.bfloat16)


def draw_norm_gain(key, part):
    key = jax.random.fold_in(key, 23)
    value_rows = jnp.clip(1.0 + 0.15 * jax.random.normal(key, (MODEL_WIDTH,), jnp.float32), 0.4, 1.6)
    return value_rows


def draw_key_weight(key, part):
    shared_weight = shared_keys(key)
    return shared_weight.astype(jnp.bfloat16)


def draw_query_weight(key, part):
    key = jax.random.fold_in(key, 37)
    own_key = jax.random.fold_in(key, 0)
    own = jnp.clip(jax.random.normal(own_key, (MODEL_WIDTH, QUERY_HEAD_SLICE * HEAD_SIZE), jnp.float32), -6.0, 6.0) / jnp.sqrt(jnp.float32(MODEL_WIDTH))
    value_rows = own
    return value_rows.astype(jnp.bfloat16)


def block_scale(stream_key, shape, cuts, least, high):
    level = 1.0
    for dim, blocks in cuts:
        draws = jax.random.uniform(jax.random.fold_in(jax.random.fold_in(stream_key, 6), dim), (blocks,), jnp.float32, least / len(cuts), high / len(cuts))
        level = level * jnp.repeat(jnp.exp(draws), shape[dim] // blocks).reshape((-1,) + (1,) * (len(shape) - 1 - dim))
    return level


def scatter_about(key, shape, deviation, bound, shards=(), held_as=jnp.bfloat16):
    factor_of = block_scale(key, shape, shards, -0.22, 0.18) if shards else 1.0
    result = jax.random.normal(key, shape, jnp.float32) * deviation * factor_of
    return jnp.minimum(jnp.maximum(result, -bound), bound).astype(held_as)


def setup_inputs(seed: int = 0) -> dict:
    key_list = jax.random.split(jax.random.key(seed), 6)
    return {
        "tokens": draw_tokens(jax.random.fold_in(key_list[5], 71), 0),
        "norm_gain": draw_norm_gain(jax.random.fold_in(key_list[5], 71), 0),
        "query_weight": draw_query_weight(jax.random.fold_in(key_list[5], 71), 0),
        "key_weight": draw_key_weight(jax.random.fold_in(key_list[5], 71), 0),
        "value_matrix": scatter_about(key_list[4], (MODEL_WIDTH, KEY_VALUE_HEADS * HEAD_SIZE), MODEL_WIDTH ** -0.5, 0.0625, ((0, 128), (1, 2))),
    }


EPS = 1e-05
THETA = 500000.0

def rotate(value_rows, positions):
    rows = value_rows.shape[0]
    heads = value_rows.shape[1] // HEAD_SIZE
    split = value_rows.reshape(rows, heads, HEAD_SIZE)
    index = jnp.arange(HEAD_SIZE // 2).astype(jnp.float32)
    freqs = jnp.exp(index * (-2.0 / HEAD_SIZE) * jnp.log(jnp.float32(THETA)))
    angles = positions[:, None] * freqs[None, :]
    cosine = jnp.cos(angles)[:, None, :]
    sine = jnp.sin(angles)[:, None, :]
    first = split[..., :HEAD_SIZE // 2]
    second = split[..., HEAD_SIZE // 2:]
    joined = jnp.concatenate([first * cosine - second * sine, second * cosine + first * sine], axis=-1)
    return joined.reshape(rows, heads * HEAD_SIZE)

def reference(tokens, norm_gain, query_weight, key_weight, value_matrix):
    group_size = QUERY_HEAD_SLICE // KEY_VALUE_HEADS

    def one_instance(states):
        floats = states.astype(jnp.float32)
        inverse = 1.0 / jnp.sqrt(lax.optimization_barrier(jnp.sum(floats * floats, axis=1)) / MODEL_WIDTH + EPS)
        scaled = (floats * norm_gain[None, :]).astype(jnp.bfloat16)
        query = jnp.dot(scaled, query_weight, preferred_element_type=jnp.float32) * inverse[:, None]
        key = jnp.dot(scaled, key_weight, preferred_element_type=jnp.float32) * inverse[:, None]
        value = jnp.dot(scaled, value_matrix, preferred_element_type=jnp.float32) * inverse[:, None]
        positions = jnp.arange(PROMPT_LENGTH).astype(jnp.float32)
        rotated_query = rotate(query, positions).astype(jnp.bfloat16)
        rotated_key_cache = rotate(key, positions).astype(jnp.bfloat16)
        value_store_cache = value.astype(jnp.bfloat16)
        query_head_rows = rotated_query.astype(jnp.float32).reshape(PROMPT_LENGTH, KEY_VALUE_HEADS, group_size, HEAD_SIZE)
        key_head_rows = rotated_key_cache.astype(jnp.float32).reshape(PROMPT_LENGTH, KEY_VALUE_HEADS, HEAD_SIZE)
        value_head_rows = value_store_cache.astype(jnp.float32).reshape(PROMPT_LENGTH, KEY_VALUE_HEADS, HEAD_SIZE)
        score = jnp.einsum('rgjd,ngd->gjrn', query_head_rows, key_head_rows) / jnp.sqrt(jnp.float32(HEAD_SIZE))
        order = jnp.arange(PROMPT_LENGTH)
        causal = order[:, None] >= order[None, :]
        score = jnp.where(causal, score, jnp.float32(-1e+30))
        top = lax.optimization_barrier(jnp.max(score, axis=-1, keepdims=True))
        expo = jnp.where(causal, jnp.exp(score - top), jnp.float32(0.0))
        total = lax.optimization_barrier(jnp.sum(expo, axis=-1))
        weight = expo.astype(jnp.bfloat16).astype(jnp.float32)
        mixed = jnp.einsum('gjrn,ngd->gjrd', weight, value_head_rows) / total[..., None]
        attended = jnp.transpose(mixed, (2, 0, 1, 3)).reshape(PROMPT_LENGTH, QUERY_HEAD_SLICE * HEAD_SIZE).astype(jnp.bfloat16)
        return (attended, rotated_key_cache, value_store_cache)
    attended, rotated_key_cache, value_store_cache = lax.map(one_instance, tokens)
    return (attended, rotated_key_cache, value_store_cache)
```

```python
import jax
import jax.numpy as jnp
from jax import lax
from jax.sharding import PartitionSpec as P

MODEL_WIDTH = 8192
HEAD_SIZE = 128


EPS = 1e-05
THETA = 500000.0


def rotate(value_rows, positions):
    rows = value_rows.shape[0]
    heads = value_rows.shape[1] // HEAD_SIZE
    split = value_rows.reshape(rows, heads, HEAD_SIZE)
    index = jnp.arange(HEAD_SIZE // 2).astype(jnp.float32)
    freqs = jnp.exp(index * (-2.0 / HEAD_SIZE) * jnp.log(jnp.float32(THETA)))
    angles = positions[:, None] * freqs[None, :]
    cosine = jnp.cos(angles)[:, None, :]
    sine = jnp.sin(angles)[:, None, :]
    first = split[..., : HEAD_SIZE // 2]
    second = split[..., HEAD_SIZE // 2 :]
    joined = jnp.concatenate(
        [first * cosine - second * sine, second * cosine + first * sine], axis=-1
    )
    return joined.reshape(rows, heads * HEAD_SIZE)


def attend_block(carry, pieces, query_heads, query_pos):
    top, total, summed = carry
    keys, value_rows = pieces
    count = keys.shape[0]
    kv_heads = keys.shape[1] // HEAD_SIZE
    key_heads = keys.reshape(count, kv_heads, HEAD_SIZE)
    value_heads = value_rows.reshape(count, kv_heads, HEAD_SIZE)
    score = jnp.einsum("rgjd,ngd->gjrn", query_heads, key_heads, preferred_element_type=jnp.float32)
    score = score / jnp.sqrt(jnp.float32(HEAD_SIZE))
    key_pos = jnp.arange(count)
    causal = query_pos[:, None] >= key_pos[None, :]
    score = jnp.where(causal, score, jnp.float32(-1e30))
    new_top = jnp.maximum(top, jnp.max(score, axis=-1))
    expo = jnp.where(causal, jnp.exp(score - new_top[..., None]), jnp.float32(0.0))
    total = jnp.sum(expo, axis=-1)
    product = jnp.einsum(
        "gjrn,ngd->gjrd", expo.astype(jnp.bfloat16), value_heads, preferred_element_type=jnp.float32
    )
    summed = product
    return (new_top, total, summed)


def local(tokens, norm_gain, query_weight, key_weight, value_matrix):
    states = tokens[0]
    seq_len = states.shape[0]
    sections = lax.axis_size("section")
    rows = seq_len // sections
    base_offset = lax.axis_index("section") * rows
    floats = states.astype(jnp.float32)
    squares = jnp.sum(floats * floats, axis=1)
    scaled = (floats * norm_gain[None, :]).astype(jnp.bfloat16)
    q_cols = query_weight.shape[1]
    kv_cols = key_weight.shape[1]
    q_heads = q_cols // HEAD_SIZE
    kv_heads = kv_cols // HEAD_SIZE
    group_size = q_heads // kv_heads
    joined = lax.all_gather(
        jnp.concatenate([query_weight, key_weight, value_matrix], axis=1), "inst", axis=0, tiled=True
    )
    part = jnp.dot(scaled, joined, preferred_element_type=jnp.float32).astype(jnp.bfloat16)
    section = lax.axis_index("section")
    marks = jnp.where(jnp.arange(HEAD_SIZE)[None, :] == section, squares[:, None], 0.0)
    part = jnp.concatenate([part, marks.astype(jnp.bfloat16)], axis=1)
    local_pos = base_offset + jnp.arange(rows)
    local_float = local_pos.astype(jnp.float32)
    total_part = lax.psum_scatter(part, "section", scatter_dimension=0, tiled=True).astype(jnp.float32)
    query = total_part[:, :q_cols]
    key = total_part[:, q_cols : q_cols + kv_cols]
    value = total_part[:, q_cols + kv_cols : q_cols + 2 * kv_cols]
    local_squares = jnp.sum(total_part[:, q_cols + 2 * kv_cols :], axis=1)
    inverse = 1.0 / jnp.sqrt(local_squares / MODEL_WIDTH + EPS)
    rotated_key_cache = rotate(key * inverse[:, None], local_float).astype(jnp.bfloat16)
    value_store_cache = (value * inverse[:, None]).astype(jnp.bfloat16)
    rotated_query = rotate(query * inverse[:, None], local_float).astype(jnp.bfloat16)
    query_heads = rotated_query.reshape(rows, kv_heads, group_size, HEAD_SIZE)
    start_carry = (
        jnp.full((kv_heads, group_size, rows), -1e30, jnp.float32),
        jnp.zeros((kv_heads, group_size, rows), jnp.float32),
        jnp.zeros((kv_heads, group_size, rows, HEAD_SIZE), jnp.float32),
    )
    both = lax.all_gather(
        jnp.concatenate([rotated_key_cache, value_store_cache], axis=1), "section", axis=0, tiled=True
    )
    top, total, summed = attend_block(
        start_carry, (both[:, :kv_cols], both[:, kv_cols:]), query_heads, local_pos
    )
    mixed = summed / total[..., None]
    attended = jnp.transpose(mixed, (2, 0, 1, 3)).reshape(rows, q_cols).astype(jnp.bfloat16)
    return (attended[None], rotated_key_cache[None], value_store_cache[None])


def solution(mesh):
    in_specs = (
        P("inst", None, "section"),
        P("section"),
        P(("section", "inst"), "tp"),
        P(("section", "inst"), "tp"),
        P(("section", "inst"), "tp"),
    )
    out_specs = (P("inst", "section", "tp"), P("inst", "section", "tp"), P("inst", "section", "tp"))
    return jax.shard_map(local, mesh=mesh, in_specs=in_specs, out_specs=out_specs, check_vma=False)
```

```python
import functools

import jax
import jax.numpy as jnp
from jax import lax
from jax.experimental import pallas as pl
from jax.experimental.pallas import tpu as pltpu
from jax.sharding import PartitionSpec as P

MODEL_WIDTH = 8192
HEAD_SIZE = 128
GROUP = 4
EPS = 1e-05
THETA = 500000.0
F32 = jnp.float32
BF16 = jnp.bfloat16
VMEM = pltpu.MemorySpace.VMEM
SMEM = pltpu.MemorySpace.SMEM
SIDE = 4
LIMIT = 40 * 1024 * 1024


def params():
    return pltpu.CompilerParams(vmem_limit_bytes=LIMIT)


def whole(count):
    return [pl.BlockSpec(memory_space=VMEM)] * count


def z_shift(array, step):
    count = lax.axis_size("section")
    return lax.ppermute(array, "section", [(i, (i + step) % count) for i in range(count)])


def xy_shift(array, dx, dy):
    pairs = [
        (x * SIDE + y, ((x + dx) % SIDE) * SIDE + (y + dy) % SIDE)
        for x in range(SIDE)
        for y in range(SIDE)
    ]
    return lax.ppermute(array, "inst", pairs)


def gather_square(shard, first, second):
    from_before = xy_shift(shard, *first)
    from_after = xy_shift(shard, -first[0], -first[1])
    from_far = xy_shift(from_before, *first)
    line = jnp.concatenate([shard, from_after, from_far, from_before], axis=0)
    half = line.shape[1] // 2
    before = xy_shift(line, *second)
    after = xy_shift(line, -second[0], -second[1])
    far_left = xy_shift(before[:, :half], *second)
    far_right = xy_shift(after[:, half:], -second[0], -second[1])
    return line, after, far_left, far_right, before


def reduce_ring(parts, lead, tail):
    up, down = lead, tail
    split = lead.shape[1]
    up = z_shift(up, 1)
    down = z_shift(down, -1)
    up = jnp.concatenate(
        [parts[3][:, :split] + up.astype(F32), parts[3][:, split:]], axis=1
    ).astype(BF16)
    down = jnp.concatenate(
        [parts[5][:, :split], parts[5][:, split:] + down.astype(F32)], axis=1
    ).astype(BF16)
    for near, far in ((2, 6), (1, 7)):
        up = z_shift(up, 1)
        down = z_shift(down, -1)
        up = (parts[near] + up.astype(F32)).astype(BF16)
        down = (parts[far] + down.astype(F32)).astype(BF16)
    return z_shift(up, 1), z_shift(down, -1)


def prepare_kernel(section_ref, token_ref, gain_ref, scaled_ref, marks_ref):
    floats = token_ref[0].astype(F32)
    scaled_ref[...] = (floats * gain_ref[...]).astype(BF16)
    squares = jnp.sum(floats * floats, axis=1, keepdims=True)
    lane = lax.broadcasted_iota(jnp.int32, marks_ref.shape, 1)
    marks_ref[...] = jnp.where(lane == section_ref[0], squares, 0.0).astype(BF16)


def prepare(section, tokens, gain, sections):
    _, seq_len, width = tokens.shape
    rows = seq_len // sections
    return pl.pallas_call(
        prepare_kernel,
        grid_spec=pltpu.PrefetchScalarGridSpec(
            num_scalar_prefetch=1,
            grid=(sections,),
            in_specs=[
                pl.BlockSpec((1, rows, width), lambda d, s: (0, (d + s[0]) % sections, 0)),
                pl.BlockSpec((1, width), lambda d, s: (0, 0)),
            ],
            out_specs=[
                pl.BlockSpec((rows, width), lambda d, s: (d, 0)),
                pl.BlockSpec((rows, HEAD_SIZE), lambda d, s: (d, 0)),
            ],
        ),
        out_shape=[
            jax.ShapeDtypeStruct((seq_len, width), BF16),
            jax.ShapeDtypeStruct((seq_len, HEAD_SIZE), BF16),
        ],
        compiler_params=params(),
    )(section, tokens, gain)


def key_value_kernel(place_ref, scaled_ref, marks_ref, *refs):
    key_blocks, value_blocks = refs[:5], refs[5:10]
    part_ref, lead_ref, tail_ref, weight = refs[10:]
    x, y = place_ref[0], place_ref[1]
    cols = key_blocks[0].shape[1]
    depth = key_blocks[0].shape[0] // SIDE
    half = cols // 2

    def place(blocks, offset, row_of):
        spots = (
            (0, blocks[0], 0, cols),
            (1, blocks[1], 0, cols),
            (2, blocks[2], 0, half),
            (2, blocks[3], half, half),
            (3, blocks[4], 0, cols),
        )
        for far, block, start, size in spots:
            for near in range(SIDE):
                row = pl.multiple_of(row_of(far, near), depth)
                weight[pl.ds(row, depth), offset + start : offset + start + size] = block[
                    near * depth : (near + 1) * depth, :
                ]

    def key_row(far, near):
        return lax.rem(x + far, SIDE) * (SIDE * depth) + lax.rem(y + near, SIDE) * depth

    def value_row(far, near):
        return lax.rem(x + near, SIDE) * (SIDE * depth) + lax.rem(y + far, SIDE) * depth

    place(key_blocks, 0, key_row)
    place(value_blocks, cols, value_row)
    step = 256
    for start in range(0, 2 * cols, step):
        part_ref[:, start : start + step] = jnp.dot(
            scaled_ref[...], weight[:, start : start + step], preferred_element_type=F32
        )
    part_ref[:, 2 * cols :] = marks_ref[...].astype(F32)
    rows = part_ref.shape[0] // 8
    split = lead_ref.shape[1]
    lead_ref[...] = part_ref[4 * rows : 5 * rows, :split].astype(BF16)
    tail_ref[...] = part_ref[4 * rows : 5 * rows, split:].astype(BF16)


def key_value_parts(place, scaled, marks, key_blocks, value_blocks):
    seq_len = scaled.shape[0]
    rows = seq_len // 8
    cols = key_blocks[0].shape[1]
    wide = 2 * cols + HEAD_SIZE
    split = cols + HEAD_SIZE
    return pl.pallas_call(
        key_value_kernel,
        in_specs=[pl.BlockSpec(memory_space=SMEM)] + whole(12),
        out_specs=whole(3),
        out_shape=[
            jax.ShapeDtypeStruct((seq_len, wide), F32),
            jax.ShapeDtypeStruct((rows, split), BF16),
            jax.ShapeDtypeStruct((rows, wide - split), BF16),
        ],
        scratch_shapes=[pltpu.VMEM((SIDE * key_blocks[0].shape[0], 2 * cols), BF16)],
        compiler_params=params(),
    )(place, scaled, marks, *key_blocks, *value_blocks)


def query_kernel(scaled_ref, weight_ref, part_ref, first_ref):
    part = jnp.dot(scaled_ref[...], weight_ref[...], preferred_element_type=F32)
    part_ref[...] = part
    rows = part_ref.shape[0] // 8
    first_ref[...] = part[4 * rows : 5 * rows].astype(BF16)


def query_parts(scaled, weight):
    seq_len, depth = scaled.shape
    cols = weight.shape[1]
    step = 256
    return pl.pallas_call(
        query_kernel,
        grid=(cols // step,),
        in_specs=[
            pl.BlockSpec((seq_len, depth), lambda i: (0, 0)),
            pl.BlockSpec((depth, step), lambda i: (0, i)),
        ],
        out_specs=[
            pl.BlockSpec((seq_len, step), lambda i: (0, i)),
            pl.BlockSpec((seq_len // 8, step), lambda i: (0, i)),
        ],
        out_shape=[
            jax.ShapeDtypeStruct((seq_len, cols), F32),
            jax.ShapeDtypeStruct((seq_len // 8, cols), BF16),
        ],
        compiler_params=params(),
    )(scaled, weight)


def turn(head, cosine, sine):
    return head * cosine + pltpu.roll(head, HEAD_SIZE // 2, 1) * sine


def finish_kernel(own_ref, up_ref, down_ref, cos_ref, sin_ref, both_ref, key_ref, value_ref, inv_ref):
    cols = key_ref.shape[2]
    total = own_ref[...] + up_ref[...].astype(F32) + down_ref[...].astype(F32)
    squares = jnp.sum(total[:, 2 * cols :], axis=1, keepdims=True)
    inverse = 1.0 / jnp.sqrt(squares / MODEL_WIDTH + EPS)
    inv_ref[...] = jnp.broadcast_to(inverse, inv_ref.shape)
    cosine, sine = cos_ref[...], sin_ref[...]
    for start in range(0, cols, HEAD_SIZE):
        span = slice(start, start + HEAD_SIZE)
        head = turn(total[:, span] * inverse, cosine, sine).astype(BF16)
        both_ref[:, span] = head
        key_ref[0, :, span] = head
    value = (total[:, cols : 2 * cols] * inverse).astype(BF16)
    both_ref[:, cols:] = value
    value_ref[0] = value


def finish_key_value(own, up, down, cosine, sine):
    rows = own.shape[0]
    cols = (own.shape[1] - HEAD_SIZE) // 2
    return pl.pallas_call(
        finish_kernel,
        in_specs=whole(5),
        out_specs=whole(4),
        out_shape=[
            jax.ShapeDtypeStruct((rows, 2 * cols), BF16),
            jax.ShapeDtypeStruct((1, rows, cols), BF16),
            jax.ShapeDtypeStruct((1, rows, cols), BF16),
            jax.ShapeDtypeStruct((rows, HEAD_SIZE), F32),
        ],
        compiler_params=params(),
    )(own, up, down, cosine, sine)


def attend_kernel(section_ref, own_ref, up_ref, down_ref, inv_ref, cos_ref, sin_ref, *refs):
    key_refs, value_refs, out_ref = refs[:8], refs[8:16], refs[16]
    section = section_ref[0]
    rows = own_ref.shape[0]
    cosine, sine, inverse = cos_ref[...], sin_ref[...], inv_ref[...]
    query_row = lax.broadcasted_iota(jnp.int32, (GROUP, rows, rows), 1).reshape(GROUP * rows, rows)
    key_col = lax.broadcasted_iota(jnp.int32, (GROUP * rows, rows), 1)
    near_mask = query_row >= key_col
    block = lax.broadcasted_iota(jnp.int32, (1, 7 * rows), 1) // rows + 1
    past_mask = section + block >= 8
    scale = 1.4426950408889634 / (HEAD_SIZE**0.5)
    low = F32(-1e30)
    heads = own_ref.shape[1] // HEAD_SIZE
    for kv_head in range(heads // GROUP):
        queries = []
        for member in range(GROUP):
            start = (kv_head * GROUP + member) * HEAD_SIZE
            span = slice(start, start + HEAD_SIZE)
            query = own_ref[:, span] + up_ref[:, span].astype(F32) + down_ref[:, span].astype(F32)
            queries.append(turn(query * inverse, cosine, sine).astype(BF16))
        query = jnp.concatenate(queries, axis=0)
        keys = jnp.concatenate(
            [ref[:, kv_head * HEAD_SIZE : (kv_head + 1) * HEAD_SIZE] for ref in key_refs], axis=0
        )
        values = jnp.concatenate(
            [
                ref[:, ref.shape[1] - (heads // GROUP - kv_head) * HEAD_SIZE :][:, :HEAD_SIZE]
                for ref in value_refs
            ],
            axis=0,
        )
        score = lax.dot_general(
            query, keys, (((1,), (1,)), ((), ())), preferred_element_type=F32
        )
        score = jnp.concatenate(
            [
                jnp.where(near_mask, score[:, :rows], low),
                jnp.where(past_mask, score[:, rows:], low),
            ],
            axis=1,
        )
        top = jnp.max(score, axis=1, keepdims=True)
        expo = jnp.exp2((score - top) * scale)
        total = jnp.sum(expo, axis=1, keepdims=True)
        mixed = jnp.dot(expo.astype(BF16), values, preferred_element_type=F32) / total
        for member in range(GROUP):
            start = (kv_head * GROUP + member) * HEAD_SIZE
            out_ref[0, :, start : start + HEAD_SIZE] = mixed[
                member * rows : (member + 1) * rows
            ].astype(BF16)


def attend(section, own, up, down, inverse, cosine, sine, key_blocks, value_blocks):
    rows, cols = own.shape
    return pl.pallas_call(
        attend_kernel,
        in_specs=[pl.BlockSpec(memory_space=SMEM)] + whole(22),
        out_specs=pl.BlockSpec(memory_space=VMEM),
        out_shape=jax.ShapeDtypeStruct((1, rows, cols), BF16),
        compiler_params=params(),
    )(section, own, up, down, inverse, cosine, sine, *key_blocks, *value_blocks)


def tables(first, rows):
    index = jnp.arange(HEAD_SIZE // 2).astype(F32)
    freqs = jnp.exp(index * (-2.0 / HEAD_SIZE) * jnp.log(F32(THETA)))
    positions = (first + jnp.arange(rows)).astype(F32)
    angles = positions[:, None] * freqs[None, :]
    cosine, sine = jnp.cos(angles), jnp.sin(angles)
    return jnp.concatenate([cosine, cosine], axis=1), jnp.concatenate([-sine, sine], axis=1)


def local(tokens, norm_gain, query_weight, key_weight, value_matrix):
    sections = lax.axis_size("section")
    rows = tokens.shape[1] // sections
    kv_cols = key_weight.shape[1]
    section = lax.axis_index("section")
    inst = lax.axis_index("inst")
    here = section.astype(jnp.int32).reshape(1)
    place = jnp.stack([inst // SIDE, inst % SIDE]).astype(jnp.int32)

    query_all = lax.all_gather(query_weight, "inst", axis=0, tiled=True)
    key_blocks = gather_square(key_weight, (0, 1), (1, 0))
    value_blocks = gather_square(value_matrix, (1, 0), (0, 1))
    scaled, marks = prepare(here, tokens, norm_gain.reshape(1, -1), sections)
    cosine, sine = tables(section * rows, rows)

    part, lead, tail = key_value_parts(place, scaled, marks, key_blocks, value_blocks)
    parts = [part[d * rows : (d + 1) * rows] for d in range(sections)]
    up, down = reduce_ring(parts, lead, tail)
    both, key_cache, value_cache, inverse = finish_key_value(parts[0], up, down, cosine, sine)

    before, after = both, both
    key_blocks, value_blocks = [both] * 8, [both] * 8
    for step in range(1, 4):
        before, after = z_shift(before, 1), z_shift(after, -1)
        key_blocks[8 - step] = value_blocks[8 - step] = before
        key_blocks[step] = value_blocks[step] = after
    key_blocks[4] = z_shift(before[:, :kv_cols], 1)
    value_blocks[4] = z_shift(after[:, kv_cols:], -1)

    part, first = query_parts(scaled, query_all)
    parts = [part[d * rows : (d + 1) * rows] for d in range(sections)]
    half = first.shape[1] // 2
    up, down = reduce_ring(parts, first[:, :half], first[:, half:])
    attended = attend(
        here, parts[0], up, down, inverse, cosine, sine, key_blocks, value_blocks
    )
    return attended, key_cache, value_cache


def solution(mesh):
    in_specs = (
        P("inst", None, "section"),
        P("section"),
        P(("section", "inst"), "tp"),
        P(("section", "inst"), "tp"),
        P(("section", "inst"), "tp"),
    )
    out_specs = (P("inst", "section", "tp"),) * 3
    return jax.shard_map(local, mesh=mesh, in_specs=in_specs, out_specs=out_specs, check_vma=False)
```

```python
import jax
import jax.numpy as jnp
from jax import lax
from jax.experimental import pallas as pl
from jax.experimental.pallas import tpu as pltpu
from jax.sharding import PartitionSpec as P

MODEL_WIDTH = 8192
HEAD_SIZE = 128
EPS = 1e-05
THETA = 500000.0
F32 = jnp.float32
BF16 = jnp.bfloat16
VMEM = pltpu.MemorySpace.VMEM
SMEM = pltpu.MemorySpace.SMEM
HBM = pltpu.MemorySpace.HBM
SECTIONS = 8
INSTS = 16
STRIPE = 32
EXTRA = 16
QUERY_COLS = 4 * HEAD_SIZE
KEY_AT = QUERY_COLS
VALUE_AT = QUERY_COLS + HEAD_SIZE
WIDE = QUERY_COLS + 2 * HEAD_SIZE


def params(mebibytes):
    return pltpu.CompilerParams(vmem_limit_bytes=mebibytes * 1024 * 1024)


def whole(count, space=VMEM):
    return [pl.BlockSpec(memory_space=space)] * count


def scalar():
    return pl.BlockSpec(memory_space=SMEM)


def z_shift(array, step):
    return lax.ppermute(array, "section", [(i, (i + step) % SECTIONS) for i in range(SECTIONS)])


def swap_cores(array):
    return lax.ppermute(array, "tp", [(0, 1), (1, 0)])


def stripe_kernel(core_ref, token_ref, gain_ref, out_ref):
    rows, width = token_ref.shape[1:]
    half = out_ref.shape[1]
    feature = lax.broadcasted_iota(jnp.int32, (width, half), 0)
    lane = lax.broadcasted_iota(jnp.int32, (width, half), 1)
    wanted = (lane // STRIPE) * (2 * STRIPE) + core_ref[0] * STRIPE + lane % STRIPE
    pick = jnp.where(feature == wanted, 1.0, 0.0).astype(BF16)
    floats = token_ref[0].astype(F32)
    scaled = (floats * gain_ref[...]).astype(BF16)
    out_ref[:rows] = jnp.dot(scaled, pick, preferred_element_type=F32).astype(BF16)
    squares = jnp.sum(floats * floats, axis=1, keepdims=True)
    squares = jnp.broadcast_to(squares, (rows, HEAD_SIZE)).T[:EXTRA]
    high = squares.astype(BF16)
    low = (squares - high.astype(F32)).astype(BF16)
    row = lax.broadcasted_iota(jnp.int32, squares.shape, 0)
    out_ref[rows:] = jnp.where(row == 0, high, jnp.where(row == 1, low, jnp.zeros_like(low)))


def stripes(core, tokens, gain):
    _, seq_len, width = tokens.shape
    rows = seq_len // 2
    run = pl.pallas_call(
        stripe_kernel,
        grid=(2,),
        in_specs=[
            scalar(),
            pl.BlockSpec((1, rows, width), lambda i: (0, i, 0)),
            pl.BlockSpec((1, width), lambda i: (0, 0)),
        ],
        out_specs=pl.BlockSpec((None, rows + EXTRA, width // 2), lambda i: (i, 0, 0)),
        out_shape=jax.ShapeDtypeStruct((2, rows + EXTRA, width // 2), BF16),
        compiler_params=params(16),
    )
    both = run(core, tokens, gain)
    return both[0], both[1]


def cut_far_kernel(before_ref, behind_ref, left_ref, right_ref):
    half = left_ref.shape[1]
    left_ref[...] = before_ref[:, :half]
    right_ref[...] = behind_ref[:, half:]


def cut_far(before, behind):
    rows, cols = before.shape
    shape = jax.ShapeDtypeStruct((rows, cols // 2), BF16)
    return pl.pallas_call(
        cut_far_kernel,
        in_specs=whole(2),
        out_specs=whole(2),
        out_shape=[shape, shape],
        cost_estimate=pl.CostEstimate(flops=57_000_000_000, transcendentals=0, bytes_accessed=2_000_000),
        compiler_params=params(8),
    )(before, behind)


def spread(block):
    blocks = [block] * SECTIONS
    before, behind = block, block
    for step in range(1, 4):
        before, behind = z_shift(before, 1), z_shift(behind, -1)
        blocks[SECTIONS - step], blocks[step] = before, behind
    left, right = cut_far(before, behind)
    return blocks[:4] + blocks[5:] + [z_shift(left, 1), z_shift(right, -1)]


def cut_kernel(core_ref, query_ref, key_ref, value_ref, keep_ref, send_ref):
    core = core_ref[0]
    for ref, first in ((keep_ref, core), (send_ref, 1 - core)):
        rows = pl.ds(pl.multiple_of(first * STRIPE, STRIPE), STRIPE)
        start = 0
        for source in (query_ref, key_ref, value_ref):
            ref[:, start : start + source.shape[1]] = source[rows, :]
            start += source.shape[1]


def sort_kernel(core_ref, keep_ref, other_ref, out_ref):
    first = core_ref[0] == 0
    keep, other = keep_ref[...], other_ref[...]
    groups = out_ref.shape[0] // 2
    for side in range(2):
        mine = first if side == 0 else jnp.logical_not(first)
        columns = jnp.where(mine, keep, other)
        for group in range(groups):
            start = 0
            for size, at in ((QUERY_COLS, 0), (HEAD_SIZE, KEY_AT), (HEAD_SIZE, VALUE_AT)):
                out_ref[side * groups + group, :, at : at + size] = columns[
                    :, start + group * size : start + (group + 1) * size
                ]
                start += groups * size


def gather_weights(core, query_weight, key_weight, value_matrix):
    cols = query_weight.shape[1] + key_weight.shape[1] + value_matrix.shape[1]
    shape = jax.ShapeDtypeStruct((STRIPE, cols), BF16)
    keep, send = pl.pallas_call(
        cut_kernel,
        in_specs=[scalar()] + whole(3),
        out_specs=whole(2),
        out_shape=[shape, shape],
        compiler_params=params(8),
    )(core, query_weight, key_weight, value_matrix)
    blocks = pl.pallas_call(
        sort_kernel,
        in_specs=[scalar()] + whole(2),
        out_specs=pl.BlockSpec(memory_space=VMEM),
        out_shape=jax.ShapeDtypeStruct((SECTIONS, STRIPE, WIDE), BF16),
        compiler_params=params(8),
    )(core, keep, swap_cores(send))
    blocks = lax.all_to_all(blocks, "section", 0, 0, tiled=True)
    everything = lax.all_gather(
        blocks.reshape(SECTIONS * STRIPE, WIDE), "inst", axis=0, tiled=True
    )
    return everything.reshape(INSTS, SECTIONS, STRIPE, WIDE)


def project_kernel(section_ref, core_ref, weight_hbm, *refs):
    count = 18
    block_hbm = refs[:count]
    mine_ref, send_ref, squares_ref, total, weight, near, far, weight_sems, block_sems = refs[count:]
    distances = (0, 7, 1, 6, 2, 5, 3, 4)
    order = {0: 0, 1: 1, 2: 2, 3: 3, 5: 4, 6: 5, 7: 6}
    loads = []
    for place, distance in enumerate(distances):
        source = lax.rem(section_ref[0] + distance, SECTIONS)
        load = [
            pltpu.make_async_copy(
                weight_hbm.at[:, source], weight.at[place], weight_sems.at[place]
            )
        ]
        if distance == 4:
            spots = [(14 + index, far.at[index]) for index in range(4)]
        else:
            first = 2 * order[distance]
            spots = [(first + half, near.at[first + half]) for half in range(2)]
        for index, target in spots:
            load.append(pltpu.make_async_copy(block_hbm[index], target, block_sems.at[index]))
        for copy in load:
            copy.start()
        loads.append(load)
    rows = total.shape[0] // 2
    half_cols = QUERY_COLS // 2
    first = core_ref[0] == 0
    squares = [0.0, 0.0]
    for place, distance in enumerate(distances):
        for copy in loads[place]:
            copy.wait()
        matrix = weight[place].reshape(INSTS * STRIPE, WIDE)
        for half in range(2):
            span = slice(half * rows, (half + 1) * rows)
            if distance == 4:
                block = jnp.concatenate([far[2 * half], far[2 * half + 1]], axis=1)
            else:
                block = near[2 * order[distance] + half]
            extra = block[rows:].astype(F32)
            squares[half] += extra[0:1] + extra[1:2]
            part = jnp.dot(block[:rows], matrix, preferred_element_type=F32)
            if place == 0:
                total[span] = part
                continue
            part += total[span]
            if distance != 4:
                total[span] = part
                continue
            low, high = part[:, :half_cols], part[:, half_cols:QUERY_COLS]
            mine_ref[span, :half_cols] = jnp.where(first, low, high)
            mine_ref[span, half_cols:] = part[:, KEY_AT:]
            send_ref[span, :half_cols] = jnp.where(first, high, low).astype(BF16)
            send_ref[span, half_cols:] = part[:, KEY_AT:].astype(BF16)
            squares_ref[span] = jnp.broadcast_to(squares[half], (HEAD_SIZE, rows)).T


def project(section, core, weight, blocks):
    rows = blocks[0].shape[0]
    shape = (2 * (rows - EXTRA), QUERY_COLS)
    return pl.pallas_call(
        project_kernel,
        in_specs=[scalar()] * 2 + whole(1 + len(blocks), HBM),
        out_specs=whole(3),
        out_shape=[
            jax.ShapeDtypeStruct(shape, F32),
            jax.ShapeDtypeStruct(shape, BF16),
            jax.ShapeDtypeStruct((shape[0], HEAD_SIZE), F32),
        ],
        scratch_shapes=[
            pltpu.VMEM((shape[0], WIDE), F32),
            pltpu.VMEM((SECTIONS, INSTS, STRIPE, WIDE), BF16),
            pltpu.VMEM((14, *blocks[0].shape), BF16),
            pltpu.VMEM((4, *blocks[-1].shape), BF16),
            pltpu.SemaphoreType.DMA((SECTIONS,)),
            pltpu.SemaphoreType.DMA((len(blocks),)),
        ],
        compiler_params=params(48),
    )(section, core, weight, *blocks)


def turn(head, cosine, sine):
    return head * cosine + pltpu.roll(head, HEAD_SIZE // 2, 1) * sine


def attend_kernel(core_ref, mine_ref, other_ref, squares_ref, cos_ref, sin_ref, out_ref, *scratch):
    key_ref, value_ref = scratch
    seq_len = mine_ref.shape[0]
    step = 256
    scale_by = 1.4426950408889634 / (HEAD_SIZE**0.5)
    low = F32(-1e30)
    near = lax.broadcasted_iota(jnp.int32, (step, step), 0) >= lax.broadcasted_iota(
        jnp.int32, (step, step), 1
    )
    for start in range(0, seq_len, step):
        span = slice(start, start + step)
        stop = start + step
        inverse = 1.0 / jnp.sqrt(squares_ref[span] / MODEL_WIDTH + EPS)
        inverse = jnp.concatenate([inverse] * (QUERY_COLS // HEAD_SIZE), axis=1)
        total = mine_ref[span] + other_ref[span].astype(F32)
        total = total * inverse
        cosine, sine = cos_ref[span], sin_ref[span]
        key = turn(total[:, 2 * HEAD_SIZE : 3 * HEAD_SIZE], cosine, sine).astype(BF16)
        value = total[:, 3 * HEAD_SIZE :].astype(BF16)
        key_ref[span] = key
        value_ref[span] = value
        out_ref[span, 2 * HEAD_SIZE :] = jnp.where(core_ref[0] == 0, key, value)
        query = jnp.concatenate(
            [
                turn(total[:, :HEAD_SIZE], cosine, sine),
                turn(total[:, HEAD_SIZE : 2 * HEAD_SIZE], cosine, sine),
            ],
            axis=0,
        ).astype(BF16)
        score = lax.dot_general(
            query, key_ref[:stop], (((1,), (1,)), ((), ())), preferred_element_type=F32
        )
        mask = jnp.concatenate([near, near], axis=0)
        last = jnp.where(mask, score[:, start:], low)
        score = jnp.concatenate([score[:, :start], last], axis=1) if start else last
        top = jnp.max(score, axis=1, keepdims=True)
        expo = jnp.exp2((score - top) * scale_by)
        weight_sum = jnp.sum(expo, axis=1, keepdims=True)
        mixed = jnp.dot(expo.astype(BF16), value_ref[:stop], preferred_element_type=F32)
        mixed = (mixed / weight_sum).astype(BF16)
        out_ref[span, :HEAD_SIZE] = mixed[:step]
        out_ref[span, HEAD_SIZE : 2 * HEAD_SIZE] = mixed[step:]


def attend(core, mine, other, squares, cosine, sine):
    seq_len = mine.shape[0]
    return pl.pallas_call(
        attend_kernel,
        in_specs=[scalar()] + whole(5),
        out_specs=pl.BlockSpec(memory_space=VMEM),
        out_shape=jax.ShapeDtypeStruct((seq_len, 3 * HEAD_SIZE), BF16),
        scratch_shapes=[pltpu.VMEM((seq_len, HEAD_SIZE), BF16)] * 2,
        compiler_params=params(24),
    )(core, mine, other, squares, cosine, sine)


def place_kernel(core_ref, own_ref, other_ref, attended_ref, key_ref, value_ref):
    first = core_ref[0] == 0
    rows = attended_ref.shape[1]
    pair = 2 * HEAD_SIZE
    for group in range(own_ref.shape[0] // rows):
        span = slice(group * rows, (group + 1) * rows)
        own, other = own_ref[span], other_ref[span]
        low, high = jnp.where(first, own, other), jnp.where(first, other, own)
        at = group * 2 * pair
        attended_ref[0, :, at : at + pair] = low[:, :pair]
        attended_ref[0, :, at + pair : at + 2 * pair] = high[:, :pair]
        columns = slice(group * HEAD_SIZE, (group + 1) * HEAD_SIZE)
        key_ref[0, :, columns] = low[:, pair:]
        value_ref[0, :, columns] = high[:, pair:]


def place(core, own, other, rows):
    groups = own.shape[0] // rows
    return pl.pallas_call(
        place_kernel,
        in_specs=[scalar()] + whole(2),
        out_specs=whole(3),
        out_shape=[
            jax.ShapeDtypeStruct((1, rows, groups * 4 * HEAD_SIZE), BF16),
            jax.ShapeDtypeStruct((1, rows, groups * HEAD_SIZE), BF16),
            jax.ShapeDtypeStruct((1, rows, groups * HEAD_SIZE), BF16),
        ],
        compiler_params=params(8),
    )(core, own, other)


def tables(rows):
    index = jnp.arange(HEAD_SIZE // 2).astype(F32)
    freqs = jnp.exp(index * (-2.0 / HEAD_SIZE) * jnp.log(F32(THETA)))
    angles = jnp.arange(rows).astype(F32)[:, None] * freqs[None, :]
    cosine, sine = jnp.cos(angles), jnp.sin(angles)
    return jnp.concatenate([cosine, cosine], axis=1), jnp.concatenate([-sine, sine], axis=1)


def local(tokens, norm_gain, query_weight, key_weight, value_matrix):
    seq_len = tokens.shape[1]
    section = lax.axis_index("section").astype(jnp.int32).reshape(1)
    core_index = lax.axis_index("tp").astype(jnp.int32)
    core = core_index.reshape(1)

    halves = stripes(core, tokens, norm_gain.reshape(1, -1))
    weight = gather_weights(core, query_weight, key_weight, value_matrix)
    cosine, sine = tables(seq_len)
    upper, lower = (spread(half) for half in halves)
    near = [block for pair in zip(upper[:7], lower[:7]) for block in pair]
    mine, send, squares = project(section, core, weight, near + upper[7:] + lower[7:])
    heads = attend(core, mine, swap_cores(send), squares, cosine, sine)

    heads = lax.all_to_all(heads, "section", 0, 0, tiled=True)
    half = seq_len // 2
    own = lax.dynamic_slice_in_dim(heads, core_index * half, half, 0)
    send = lax.dynamic_slice_in_dim(heads, (1 - core_index) * half, half, 0)
    return place(core, own, swap_cores(send), seq_len // SECTIONS)


def solution(mesh):
    in_specs = (
        P("inst", None, "section"),
        P("section"),
        P(("section", "inst"), "tp"),
        P(("section", "inst"), "tp"),
        P(("section", "inst"), "tp"),
    )
    out_specs = (P("inst", "section", "tp"),) * 3
    return jax.shard_map(local, mesh=mesh, in_specs=in_specs, out_specs=out_specs, check_vma=False)
```

```python
import jax
import jax.numpy as jnp
from jax import lax
from jax.experimental import pallas as pl
from jax.experimental.pallas import tpu as pltpu
from jax.sharding import PartitionSpec as P

MODEL_WIDTH = 8192
HEAD_SIZE = 128
EPS = 1e-05
THETA = 500000.0
F32 = jnp.float32
BF16 = jnp.bfloat16
VMEM = pltpu.MemorySpace.VMEM
SMEM = pltpu.MemorySpace.SMEM
HBM = pltpu.MemorySpace.HBM
SECTIONS = 8
INSTS = 16
STRIPE = 32
EXTRA = 16
QUERY_COLS = 4 * HEAD_SIZE
KEY_AT = QUERY_COLS
VALUE_AT = QUERY_COLS + HEAD_SIZE
WIDE = QUERY_COLS + 2 * HEAD_SIZE


def params(mebibytes):
    return pltpu.CompilerParams(vmem_limit_bytes=mebibytes * 1024 * 1024)


def whole(count, space=VMEM):
    return [pl.BlockSpec(memory_space=space)] * count


def scalar():
    return pl.BlockSpec(memory_space=SMEM)


def z_shift(array, step):
    return lax.ppermute(array, "section", [(i, (i + step) % SECTIONS) for i in range(SECTIONS)])


def swap_cores(array):
    return lax.ppermute(array, "tp", [(0, 1), (1, 0)])


def stripe_kernel(core_ref, token_ref, gain_ref, *out_refs):
    width, half = token_ref.shape[2], out_refs[0].shape[1]
    rows = token_ref.shape[1] // 2
    feature = lax.broadcasted_iota(jnp.int32, (width, half), 0)
    lane = lax.broadcasted_iota(jnp.int32, (width, half), 1)
    wanted = (lane // STRIPE) * (2 * STRIPE) + core_ref[0] * STRIPE + lane % STRIPE
    pick = jnp.where(feature == wanted, 1.0, 0.0).astype(BF16)
    for index, out_ref in enumerate(out_refs):
        floats = token_ref[0, index * rows : (index + 1) * rows].astype(F32)
        scaled = (floats * gain_ref[...]).astype(BF16)
        out_ref[:rows] = jnp.dot(scaled, pick, preferred_element_type=F32).astype(BF16)
        squares = jnp.sum(floats * floats, axis=1, keepdims=True)
        squares = jnp.broadcast_to(squares, (rows, HEAD_SIZE)).T[:EXTRA]
        high = squares.astype(BF16)
        low = (squares - high.astype(F32)).astype(BF16)
        row = lax.broadcasted_iota(jnp.int32, squares.shape, 0)
        out_ref[rows:] = jnp.where(row == 0, high, jnp.where(row == 1, low, jnp.zeros_like(low)))


def stripes(core, tokens, gain):
    _, seq_len, width = tokens.shape
    shape = jax.ShapeDtypeStruct((seq_len // 2 + EXTRA, width // 2), BF16)
    return pl.pallas_call(
        stripe_kernel,
        in_specs=[scalar()] + whole(2),
        out_specs=whole(2),
        out_shape=[shape, shape],
        compiler_params=params(20),
    )(core, tokens, gain)


def cut_far_kernel(before_ref, behind_ref, left_ref, right_ref):
    half = left_ref.shape[1]
    left_ref[...] = before_ref[:, :half]
    right_ref[...] = behind_ref[:, half:]


def cut_far(before, behind):
    rows, cols = before.shape
    shape = jax.ShapeDtypeStruct((rows, cols // 2), BF16)
    return pl.pallas_call(
        cut_far_kernel,
        in_specs=whole(2),
        out_specs=whole(2),
        out_shape=[shape, shape],
        cost_estimate=pl.CostEstimate(flops=55_000_000_000, transcendentals=0, bytes_accessed=2_000_000),
        compiler_params=params(8),
    )(before, behind)


def spread(block):
    blocks = [block] * SECTIONS
    before, behind = block, block
    for step in range(1, 4):
        before, behind = z_shift(before, 1), z_shift(behind, -1)
        blocks[SECTIONS - step], blocks[step] = before, behind
    left, right = cut_far(before, behind)
    return [blocks[d] for d in NEAR], [z_shift(left, 1), z_shift(right, -1)]


def cut_kernel(core_ref, query_ref, key_ref, value_ref, keep_ref, send_ref):
    core = core_ref[0]
    for ref, first in ((keep_ref, core), (send_ref, 1 - core)):
        rows = pl.ds(pl.multiple_of(first * STRIPE, STRIPE), STRIPE)
        start = 0
        for source in (query_ref, key_ref, value_ref):
            ref[:, start : start + source.shape[1]] = source[rows, :]
            start += source.shape[1]


def sort_kernel(core_ref, keep_ref, other_ref, out_ref):
    first = core_ref[0] == 0
    keep, other = keep_ref[...], other_ref[...]
    groups = out_ref.shape[0] // 2
    for side in range(2):
        mine = first if side == 0 else jnp.logical_not(first)
        columns = jnp.where(mine, keep, other)
        for group in range(groups):
            start = 0
            for size, at in ((QUERY_COLS, 0), (HEAD_SIZE, KEY_AT), (HEAD_SIZE, VALUE_AT)):
                out_ref[side * groups + group, :, at : at + size] = columns[
                    :, start + group * size : start + (group + 1) * size
                ]
                start += groups * size


def gather_weights(core, query_weight, key_weight, value_matrix):
    cols = query_weight.shape[1] + key_weight.shape[1] + value_matrix.shape[1]
    shape = jax.ShapeDtypeStruct((STRIPE, cols), BF16)
    keep, send = pl.pallas_call(
        cut_kernel,
        in_specs=[scalar()] + whole(3),
        out_specs=whole(2),
        out_shape=[shape, shape],
        compiler_params=params(8),
    )(core, query_weight, key_weight, value_matrix)
    blocks = pl.pallas_call(
        sort_kernel,
        in_specs=[scalar()] + whole(2),
        out_specs=pl.BlockSpec(memory_space=VMEM),
        out_shape=jax.ShapeDtypeStruct((SECTIONS, STRIPE, WIDE), BF16),
        compiler_params=params(8),
    )(core, keep, swap_cores(send))
    blocks = lax.all_to_all(blocks, "section", 0, 0, tiled=True)
    everything = lax.all_gather(
        blocks.reshape(SECTIONS * STRIPE, WIDE), "inst", axis=0, tiled=True
    )
    return everything.reshape(INSTS, SECTIONS, STRIPE, WIDE)


NEAR = (0, 1, 7, 2, 6, 3, 5)


def add_squares(squares, extra):
    extra = extra.astype(F32)
    return squares + extra[0:1] + extra[1:2]


def near_kernel(section_ref, weight_hbm, *refs):
    block_hbm = refs[:14]
    total_ref, squares_ref, weight, blocks, total, weight_sems, block_sems = refs[14:]
    loads = []
    for place, distance in enumerate(NEAR):
        source = lax.rem(section_ref[0] + distance, SECTIONS)
        load = [
            pltpu.make_async_copy(
                weight_hbm.at[:, source], weight.at[place], weight_sems.at[place]
            )
        ]
        for index in (2 * place, 2 * place + 1):
            load.append(
                pltpu.make_async_copy(block_hbm[index], blocks.at[index], block_sems.at[index])
            )
        loads.append(load)
    ahead = 2
    for load in loads[:ahead]:
        for copy in load:
            copy.start()
    rows = total_ref.shape[0] // 2
    width = block_hbm[0].shape[1]
    squares = [jnp.zeros((1, width), F32)] * 2
    for place in range(len(NEAR)):
        for copy in loads[place]:
            copy.wait()
        if place + ahead < len(NEAR):
            for copy in loads[place + ahead]:
                copy.start()
        matrix = weight[place].reshape(INSTS * STRIPE, WIDE)
        for half in range(2):
            span = slice(half * rows, (half + 1) * rows)
            block = blocks.at[2 * place + half]
            part = jnp.dot(block[:rows], matrix, preferred_element_type=F32)
            squares[half] = add_squares(squares[half], block[rows:])
            if place == 0:
                total[span] = part
            elif place + 1 < len(NEAR):
                total[span] += part
            else:
                total_ref[span] = (part + total[span]).astype(BF16)
    for half in range(2):
        squares_ref[half * 8 : (half + 1) * 8] = jnp.broadcast_to(squares[half], (8, width))


def near_sum(section, weight, blocks):
    rows, width = blocks[0].shape
    seq_len = 2 * (rows - EXTRA)
    return pl.pallas_call(
        near_kernel,
        in_specs=[scalar()] + whole(1 + len(blocks), HBM),
        out_specs=whole(2),
        out_shape=[
            jax.ShapeDtypeStruct((seq_len, WIDE), BF16),
            jax.ShapeDtypeStruct((16, width), F32),
        ],
        scratch_shapes=[
            pltpu.VMEM((len(NEAR), INSTS, STRIPE, WIDE), BF16),
            pltpu.VMEM((len(blocks), *blocks[0].shape), BF16),
            pltpu.VMEM((seq_len, WIDE), F32),
            pltpu.SemaphoreType.DMA((len(NEAR),)),
            pltpu.SemaphoreType.DMA((len(blocks),)),
        ],
        compiler_params=params(60),
    )(section, weight, *blocks)


def far_kernel(section_ref, core_ref, weight_hbm, total_hbm, sums_ref, *refs):
    block_hbm = refs[:4]
    mine_hbm, send_hbm, squares_ref = refs[4:7]
    weight, total, blocks, out, sems, block_sems, out_sems = refs[7:]
    rows = total.shape[1]
    source = lax.rem(section_ref[0] + SECTIONS // 2, SECTIONS)
    load = pltpu.make_async_copy(weight_hbm.at[:, source], weight, sems.at[2])
    load.start()
    loads = []
    for half in range(2):
        span = slice(half * rows, (half + 1) * rows)
        group = [pltpu.make_async_copy(total_hbm.at[span], total.at[half], sems.at[half])]
        for index in (2 * half, 2 * half + 1):
            group.append(
                pltpu.make_async_copy(block_hbm[index], blocks.at[index], block_sems.at[index])
            )
        for copy in group:
            copy.start()
        loads.append(group)
    load.wait()
    matrix = weight[...].reshape(INSTS * STRIPE, WIDE)
    half_cols = QUERY_COLS // 2
    first = core_ref[0] == 0
    stores = []
    for half in range(2):
        span = slice(half * rows, (half + 1) * rows)
        for copy in loads[half]:
            copy.wait()
        block = jnp.concatenate([blocks[2 * half], blocks[2 * half + 1]], axis=1)
        part = jnp.dot(block[:rows], matrix, preferred_element_type=F32)
        part = (part + total[half].astype(F32)).astype(BF16)
        low, high = part[:, :half_cols], part[:, half_cols:QUERY_COLS]
        both = part[:, KEY_AT:]
        for side, (query, target) in enumerate(
            (
                (jnp.where(first, high, low), send_hbm),
                (jnp.where(first, low, high), mine_hbm),
            )
        ):
            index = 2 * half + side
            out[index, :, :half_cols] = query
            out[index, :, half_cols:] = both
            store = pltpu.make_async_copy(out.at[index], target.at[span], out_sems.at[index])
            store.start()
            stores.append(store)
        at = slice(half * 8, (half + 1) * 8)
        squares_ref[at] = add_squares(sums_ref[at], block[rows:])
    for store in stores:
        store.wait()


def far_sum(section, core, weight, total, sums, blocks):
    seq_len = total.shape[0]
    rows = seq_len // 2
    shape = jax.ShapeDtypeStruct((seq_len, QUERY_COLS), BF16)
    return pl.pallas_call(
        far_kernel,
        in_specs=[scalar()] * 2 + whole(2, HBM) + whole(1) + whole(len(blocks), HBM),
        out_specs=whole(2, HBM) + whole(1),
        out_shape=[shape, shape, jax.ShapeDtypeStruct(sums.shape, F32)],
        scratch_shapes=[
            pltpu.VMEM((INSTS, STRIPE, WIDE), BF16),
            pltpu.VMEM((2, rows, WIDE), BF16),
            pltpu.VMEM((4, *blocks[0].shape), BF16),
            pltpu.VMEM((4, rows, QUERY_COLS), BF16),
            pltpu.SemaphoreType.DMA((3,)),
            pltpu.SemaphoreType.DMA((4,)),
            pltpu.SemaphoreType.DMA((4,)),
        ],
        compiler_params=params(60),
    )(section, core, weight, total, sums, *blocks)


def turn(head, cosine, sine):
    return head * cosine + pltpu.roll(head, HEAD_SIZE // 2, 1) * sine


def attend_kernel(
    section_ref, core_ref, mine_ref, other_ref, squares_ref, cos_ref, sin_ref, *refs
):
    piece_refs, (out_ref, key_ref, value_ref) = refs[:SECTIONS], refs[SECTIONS:]
    seq_len = mine_ref.shape[0]
    step = 256
    scale_by = 1.4426950408889634 / (HEAD_SIZE**0.5)
    low = F32(-1e30)
    near = lax.broadcasted_iota(jnp.int32, (step, step), 0) >= lax.broadcasted_iota(
        jnp.int32, (step, step), 1
    )
    for start in range(0, seq_len, step):
        span = slice(start, start + step)
        stop = start + step
        half = squares_ref.shape[1]
        at = start // half * 8
        squares = squares_ref[at : at + 1, start % half : start % half + step]
        inverse = 1.0 / jnp.sqrt(squares / MODEL_WIDTH + EPS)
        inverse = jnp.broadcast_to(inverse, (HEAD_SIZE, step)).T
        inverse = jnp.concatenate([inverse] * (QUERY_COLS // HEAD_SIZE), axis=1)
        total = mine_ref[span].astype(F32) + other_ref[span].astype(F32)
        total = total * inverse
        cosine, sine = cos_ref[span], sin_ref[span]
        key = turn(total[:, 2 * HEAD_SIZE : 3 * HEAD_SIZE], cosine, sine).astype(BF16)
        value = total[:, 3 * HEAD_SIZE :].astype(BF16)
        key_ref[span] = key
        value_ref[span] = value
        out_ref[span, 2 * HEAD_SIZE :] = jnp.where(core_ref[0] == 0, key, value)
        query = jnp.concatenate(
            [
                turn(total[:, :HEAD_SIZE], cosine, sine),
                turn(total[:, HEAD_SIZE : 2 * HEAD_SIZE], cosine, sine),
            ],
            axis=0,
        ).astype(BF16)
        score = lax.dot_general(
            query, key_ref[:stop], (((1,), (1,)), ((), ())), preferred_element_type=F32
        )
        mask = jnp.concatenate([near, near], axis=0)
        last = jnp.where(mask, score[:, start:], low)
        score = jnp.concatenate([score[:, :start], last], axis=1) if start else last
        top = jnp.max(score, axis=1, keepdims=True)
        expo = jnp.exp2((score - top) * scale_by)
        weight_sum = jnp.sum(expo, axis=1, keepdims=True)
        mixed = jnp.dot(expo.astype(BF16), value_ref[:stop], preferred_element_type=F32)
        mixed = (mixed / weight_sum).astype(BF16)
        out_ref[span, :HEAD_SIZE] = mixed[:step]
        out_ref[span, HEAD_SIZE : 2 * HEAD_SIZE] = mixed[step:]


    rows = piece_refs[0].shape[0]
    for turn_of, piece_ref in enumerate(piece_refs):
        target = lax.rem(section_ref[0] + turn_of + 4 * core_ref[0], SECTIONS)
        piece_ref[...] = out_ref[pl.ds(pl.multiple_of(target * rows, rows), rows)]


def attend(section, core, mine, other, squares, cosine, sine):
    seq_len = mine.shape[0]
    shape = (seq_len, 3 * HEAD_SIZE)
    piece = jax.ShapeDtypeStruct((seq_len // SECTIONS, shape[1]), BF16)
    return pl.pallas_call(
        attend_kernel,
        in_specs=[scalar()] * 2 + whole(5),
        out_specs=whole(SECTIONS),
        out_shape=[piece] * SECTIONS,
        scratch_shapes=[pltpu.VMEM(shape, BF16)] + [pltpu.VMEM((seq_len, HEAD_SIZE), BF16)] * 2,
        compiler_params=params(24),
    )(section, core, mine, other, squares, cosine, sine)


def send_rows(pieces):
    arrived = []
    for turn_of, piece in enumerate(pieces):
        pairs = [
            (2 * s + c, 2 * ((s + turn_of + 4 * c) % SECTIONS) + s // 4)
            for s in range(SECTIONS)
            for c in range(2)
        ]
        arrived.append(lax.ppermute(piece, ("section", "tp"), pairs))
    return arrived


def place_kernel(section_ref, core_ref, *refs):
    arrived = refs[:SECTIONS]
    attended_ref, key_ref, value_ref, pair_sems, head_sems = refs[SECTIONS:]
    pair = 2 * HEAD_SIZE
    copies = []
    for turn_of, piece in enumerate(arrived):
        source = lax.rem(section_ref[0] + SECTIONS - turn_of, SECTIONS)
        group = lax.rem(source, 4)
        from_first = source // 4 == core_ref[0]
        at = group * (2 * pair) + jnp.where(from_first, 0, pair)
        copy = pltpu.make_async_copy(
            piece.at[:, :pair],
            attended_ref.at[0, :, pl.ds(pl.multiple_of(at, HEAD_SIZE), pair)],
            pair_sems.at[turn_of],
        )
        copy.start()
        columns = pl.ds(pl.multiple_of(group * HEAD_SIZE, HEAD_SIZE), HEAD_SIZE)
        to_key = pltpu.make_async_copy(
            piece.at[:, pair:], key_ref.at[0, :, columns], head_sems.at[turn_of]
        )
        to_value = pltpu.make_async_copy(
            piece.at[:, pair:], value_ref.at[0, :, columns], head_sems.at[turn_of]
        )
        pl.when(from_first)(to_key.start)
        pl.when(jnp.logical_not(from_first))(to_value.start)
        copies.append((copy, to_key, to_value, from_first))
    for copy, to_key, to_value, from_first in copies:
        copy.wait()
        pl.when(from_first)(to_key.wait)
        pl.when(jnp.logical_not(from_first))(to_value.wait)


def place(section, core, arrived):
    rows = arrived[0].shape[0]
    return pl.pallas_call(
        place_kernel,
        in_specs=[scalar()] * 2 + whole(SECTIONS, pl.ANY),
        out_specs=whole(3, pl.ANY),
        out_shape=[
            jax.ShapeDtypeStruct((1, rows, 16 * HEAD_SIZE), BF16),
            jax.ShapeDtypeStruct((1, rows, 4 * HEAD_SIZE), BF16),
            jax.ShapeDtypeStruct((1, rows, 4 * HEAD_SIZE), BF16),
        ],
        scratch_shapes=[pltpu.SemaphoreType.DMA((SECTIONS,))] * 2,
        compiler_params=params(8),
    )(section, core, *arrived)


def tables(rows):
    index = jnp.arange(HEAD_SIZE // 2).astype(F32)
    freqs = jnp.exp(index * (-2.0 / HEAD_SIZE) * jnp.log(F32(THETA)))
    angles = jnp.arange(rows).astype(F32)[:, None] * freqs[None, :]
    cosine, sine = jnp.cos(angles), jnp.sin(angles)
    return jnp.concatenate([cosine, cosine], axis=1), jnp.concatenate([-sine, sine], axis=1)


def local(tokens, norm_gain, query_weight, key_weight, value_matrix):
    seq_len = tokens.shape[1]
    section = lax.axis_index("section").astype(jnp.int32).reshape(1)
    core_index = lax.axis_index("tp").astype(jnp.int32)
    core = core_index.reshape(1)

    halves = stripes(core, tokens, norm_gain.reshape(1, -1))
    weight = gather_weights(core, query_weight, key_weight, value_matrix)
    cosine, sine = tables(seq_len)
    (upper, upper_far), (lower, lower_far) = (spread(half) for half in halves)
    near = [block for pair in zip(upper, lower) for block in pair]
    total, sums = near_sum(section, weight, near)
    mine, send, squares = far_sum(section, core, weight, total, sums, upper_far + lower_far)
    pieces = attend(section, core, mine, swap_cores(send), squares, cosine, sine)
    return place(section, core, send_rows(pieces))


def solution(mesh):
    in_specs = (
        P("inst", None, "section"),
        P("section"),
        P(("section", "inst"), "tp"),
        P(("section", "inst"), "tp"),
        P(("section", "inst"), "tp"),
    )
    out_specs = (P("inst", "section", "tp"),) * 3
    return jax.shard_map(local, mesh=mesh, in_specs=in_specs, out_specs=out_specs, check_vma=False)
```

```python
import functools

import jax
import jax.numpy as jnp
from jax import lax
from jax.experimental import pallas as pl
from jax.experimental.pallas import tpu as pltpu
from jax.sharding import PartitionSpec as P

MODEL_WIDTH = 8192
HEAD_SIZE = 128
EPS = 1e-05
THETA = 500000.0
F32 = jnp.float32
BF16 = jnp.bfloat16
VMEM = pltpu.MemorySpace.VMEM
SMEM = pltpu.MemorySpace.SMEM
HBM = pltpu.MemorySpace.HBM
SECTIONS = 8
INSTS = 16
STRIPE = 32
EXTRA = 16
QUERY_COLS = 4 * HEAD_SIZE
KEY_AT = QUERY_COLS
VALUE_AT = QUERY_COLS + HEAD_SIZE
WIDE = QUERY_COLS + 2 * HEAD_SIZE


def params(mebibytes):
    return pltpu.CompilerParams(vmem_limit_bytes=mebibytes * 1024 * 1024)


def whole(count, space=VMEM):
    return [pl.BlockSpec(memory_space=space)] * count


def scalar():
    return pl.BlockSpec(memory_space=SMEM)


def z_shift(array, step):
    return lax.ppermute(array, "section", [(i, (i + step) % SECTIONS) for i in range(SECTIONS)])


def swap_cores(array):
    return lax.ppermute(array, "tp", [(0, 1), (1, 0)])


def stripe_kernel(core_ref, token_ref, gain_ref, *out_refs):
    width, half = token_ref.shape[2], out_refs[0].shape[1]
    rows = token_ref.shape[1] // 2
    feature = lax.broadcasted_iota(jnp.int32, (width, half), 0)
    lane = lax.broadcasted_iota(jnp.int32, (width, half), 1)
    wanted = (lane // STRIPE) * (2 * STRIPE) + core_ref[0] * STRIPE + lane % STRIPE
    pick = jnp.where(feature == wanted, 1.0, 0.0).astype(BF16)
    for index, out_ref in enumerate(out_refs):
        floats = token_ref[0, index * rows : (index + 1) * rows].astype(F32)
        scaled = (floats * gain_ref[...]).astype(BF16)
        out_ref[:rows] = jnp.dot(scaled, pick, preferred_element_type=F32).astype(BF16)
        squares = jnp.sum(floats * floats, axis=1, keepdims=True)
        squares = jnp.broadcast_to(squares, (rows, HEAD_SIZE)).T[:EXTRA]
        high = squares.astype(BF16)
        low = (squares - high.astype(F32)).astype(BF16)
        row = lax.broadcasted_iota(jnp.int32, squares.shape, 0)
        out_ref[rows:] = jnp.where(row == 0, high, jnp.where(row == 1, low, jnp.zeros_like(low)))


def stripes(core, tokens, gain):
    _, seq_len, width = tokens.shape
    shape = jax.ShapeDtypeStruct((seq_len // 2 + EXTRA, width // 2), BF16)
    return pl.pallas_call(
        stripe_kernel,
        in_specs=[scalar()] + whole(2),
        out_specs=whole(2),
        out_shape=[shape, shape],
        compiler_params=params(20),
    )(core, tokens, gain)


def cut_far_kernel(before_ref, behind_ref, left_ref, right_ref):
    half = left_ref.shape[1]
    left_ref[...] = before_ref[:, :half]
    right_ref[...] = behind_ref[:, half:]


def cut_far(before, behind):
    rows, cols = before.shape
    shape = jax.ShapeDtypeStruct((rows, cols // 2), BF16)
    return pl.pallas_call(
        cut_far_kernel,
        in_specs=whole(2),
        out_specs=whole(2),
        out_shape=[shape, shape],
        cost_estimate=pl.CostEstimate(flops=55_000_000_000, transcendentals=0, bytes_accessed=2_000_000),
        compiler_params=params(8),
    )(before, behind)


def spread(block):
    blocks = [block] * SECTIONS
    before, behind = block, block
    for step in range(1, 4):
        before, behind = z_shift(before, 1), z_shift(behind, -1)
        blocks[SECTIONS - step], blocks[step] = before, behind
    left, right = cut_far(before, behind)
    return [blocks[d] for d in NEAR], [z_shift(left, 1), z_shift(right, -1)]


def cut_kernel(core_ref, query_ref, key_ref, value_ref, keep_ref, send_ref):
    core = core_ref[0]
    for ref, first in ((keep_ref, core), (send_ref, 1 - core)):
        rows = pl.ds(pl.multiple_of(first * STRIPE, STRIPE), STRIPE)
        start = 0
        for source in (query_ref, key_ref, value_ref):
            ref[:, start : start + source.shape[1]] = source[rows, :]
            start += source.shape[1]


def sort_kernel(core_ref, keep_ref, other_ref, out_ref):
    first = core_ref[0] == 0
    keep, other = keep_ref[...], other_ref[...]
    groups = out_ref.shape[0] // 2
    for side in range(2):
        mine = first if side == 0 else jnp.logical_not(first)
        columns = jnp.where(mine, keep, other)
        for group in range(groups):
            start = 0
            for size, at in ((QUERY_COLS, 0), (HEAD_SIZE, KEY_AT), (HEAD_SIZE, VALUE_AT)):
                out_ref[side * groups + group, :, at : at + size] = columns[
                    :, start + group * size : start + (group + 1) * size
                ]
                start += groups * size


def gather_weights(core, query_weight, key_weight, value_matrix):
    cols = query_weight.shape[1] + key_weight.shape[1] + value_matrix.shape[1]
    shape = jax.ShapeDtypeStruct((STRIPE, cols), BF16)
    keep, send = pl.pallas_call(
        cut_kernel,
        in_specs=[scalar()] + whole(3),
        out_specs=whole(2),
        out_shape=[shape, shape],
        compiler_params=params(8),
    )(core, query_weight, key_weight, value_matrix)
    blocks = pl.pallas_call(
        sort_kernel,
        in_specs=[scalar()] + whole(2),
        out_specs=pl.BlockSpec(memory_space=VMEM),
        out_shape=jax.ShapeDtypeStruct((SECTIONS, STRIPE, WIDE), BF16),
        compiler_params=params(8),
    )(core, keep, swap_cores(send))
    blocks = lax.all_to_all(blocks, "section", 0, 0, tiled=True)
    everything = lax.all_gather(
        blocks.reshape(SECTIONS * STRIPE, WIDE), "inst", axis=0, tiled=True
    )
    return everything.reshape(INSTS, SECTIONS, STRIPE, WIDE)


NEAR = (0, 1, 7, 2, 6, 3, 5)


def add_squares(squares, extra):
    extra = extra.astype(F32)
    return squares + extra[0:1] + extra[1:2]


def near_kernel(section_ref, weight_hbm, *refs):
    block_hbm = refs[:14]
    total_ref, squares_ref, weight, blocks, total, weight_sems, block_sems = refs[14:]
    loads = []
    for place, distance in enumerate(NEAR):
        source = lax.rem(section_ref[0] + distance, SECTIONS)
        load = [
            pltpu.make_async_copy(
                weight_hbm.at[:, source], weight.at[place], weight_sems.at[place]
            )
        ]
        for index in (2 * place, 2 * place + 1):
            load.append(
                pltpu.make_async_copy(block_hbm[index], blocks.at[index], block_sems.at[index])
            )
        loads.append(load)
    ahead = 2
    for load in loads[:ahead]:
        for copy in load:
            copy.start()
    rows = total_ref.shape[0] // 2
    width = block_hbm[0].shape[1]
    squares = [jnp.zeros((1, width), F32)] * 2
    for place in range(len(NEAR)):
        for copy in loads[place]:
            copy.wait()
        if place + ahead < len(NEAR):
            for copy in loads[place + ahead]:
                copy.start()
        matrix = weight[place].reshape(INSTS * STRIPE, WIDE)
        for half in range(2):
            span = slice(half * rows, (half + 1) * rows)
            block = blocks.at[2 * place + half]
            part = jnp.dot(block[:rows], matrix, preferred_element_type=F32)
            squares[half] = add_squares(squares[half], block[rows:])
            if place == 0:
                total[span] = part
            elif place + 1 < len(NEAR):
                total[span] += part
            else:
                total_ref[span] = (part + total[span]).astype(BF16)
    for half in range(2):
        squares_ref[half * 8 : (half + 1) * 8] = jnp.broadcast_to(squares[half], (8, width))


def near_sum(section, weight, blocks):
    rows, width = blocks[0].shape
    seq_len = 2 * (rows - EXTRA)
    return pl.pallas_call(
        near_kernel,
        in_specs=[scalar()] + whole(1 + len(blocks), HBM),
        out_specs=whole(2),
        out_shape=[
            jax.ShapeDtypeStruct((seq_len, WIDE), BF16),
            jax.ShapeDtypeStruct((16, width), F32),
        ],
        scratch_shapes=[
            pltpu.VMEM((len(NEAR), INSTS, STRIPE, WIDE), BF16),
            pltpu.VMEM((len(blocks), *blocks[0].shape), BF16),
            pltpu.VMEM((seq_len, WIDE), F32),
            pltpu.SemaphoreType.DMA((len(NEAR),)),
            pltpu.SemaphoreType.DMA((len(blocks),)),
        ],
        compiler_params=params(60),
    )(section, weight, *blocks)


OFFSETS = (0, 5, 2, 7)


def target_rows(section, core, turn_of, rows):
    target = lax.rem(section + OFFSETS[turn_of] + 4 * core, SECTIONS)
    return pl.ds(pl.multiple_of(target * rows, rows), rows)


def far_kernel(section_ref, core_ref, weight_hbm, total_hbm, sums_ref, *refs):
    block_hbm = refs[:4]
    mine_hbm, send_hbm, pair_hbm, squares_ref = refs[4:8]
    weight, total, blocks, out, sems, block_sems, out_sems = refs[8:]
    rows = total.shape[1]
    source = lax.rem(section_ref[0] + SECTIONS // 2, SECTIONS)
    load = pltpu.make_async_copy(weight_hbm.at[:, source], weight, sems.at[2])
    load.start()
    loads = []
    for half in range(2):
        span = slice(half * rows, (half + 1) * rows)
        group = [pltpu.make_async_copy(total_hbm.at[span], total.at[half], sems.at[half])]
        for index in (2 * half, 2 * half + 1):
            group.append(
                pltpu.make_async_copy(block_hbm[index], blocks.at[index], block_sems.at[index])
            )
        for copy in group:
            copy.start()
        loads.append(group)
    load.wait()
    matrix = weight[...].reshape(INSTS * STRIPE, WIDE)
    stores = []
    for half in range(2):
        span = slice(half * rows, (half + 1) * rows)
        for copy in loads[half]:
            copy.wait()
        block = jnp.concatenate([blocks[2 * half], blocks[2 * half + 1]], axis=1)
        part = jnp.dot(block[:rows], matrix, preferred_element_type=F32)
        out[span] = (part + total[half].astype(F32)).astype(BF16)
        at = slice(half * 8, (half + 1) * 8)
        squares_ref[at] = add_squares(sums_ref[at], block[rows:])
        store = pltpu.make_async_copy(
            out.at[span, QUERY_COLS:], pair_hbm.at[span], out_sems.at[half]
        )
        store.start()
        stores.append(store)
    chunk = 2 * rows // SECTIONS
    for core, target in ((1 - core_ref[0], send_hbm), (core_ref[0], mine_hbm)):
        for turn_of in range(4):
            store = pltpu.make_async_copy(
                out.at[target_rows(section_ref[0], core, turn_of, chunk), :QUERY_COLS],
                target.at[turn_of * chunk : (turn_of + 1) * chunk],
                out_sems.at[len(stores)],
            )
            store.start()
            stores.append(store)
    for store in stores:
        store.wait()


def far_sum(section, core, weight, total, sums, blocks):
    seq_len = total.shape[0]
    rows = seq_len // 2
    queries = jax.ShapeDtypeStruct((rows, QUERY_COLS), BF16)
    return pl.pallas_call(
        far_kernel,
        in_specs=[scalar()] * 2 + whole(2, HBM) + whole(1) + whole(len(blocks), HBM),
        out_specs=whole(3, HBM) + whole(1),
        out_shape=[
            queries,
            queries,
            jax.ShapeDtypeStruct((seq_len, WIDE - QUERY_COLS), BF16),
            jax.ShapeDtypeStruct(sums.shape, F32),
        ],
        scratch_shapes=[
            pltpu.VMEM((INSTS, STRIPE, WIDE), BF16),
            pltpu.VMEM((2, rows, WIDE), BF16),
            pltpu.VMEM((4, *blocks[0].shape), BF16),
            pltpu.VMEM((seq_len, WIDE), BF16),
            pltpu.SemaphoreType.DMA((3,)),
            pltpu.SemaphoreType.DMA((4,)),
            pltpu.SemaphoreType.DMA((10,)),
        ],
        compiler_params=params(60),
    )(section, core, weight, total, sums, *blocks)


def turn(head, cosine, sine):
    return head * cosine + pltpu.roll(head, HEAD_SIZE // 2, 1) * sine


def prepare_keys(mine, other, squares_ref, cos_ref, sin_ref, key_ref, value_ref, inverse_ref):
    step = 256
    half = squares_ref.shape[1]
    for start in range(0, key_ref.shape[0], step):
        span = slice(start, start + step)
        at = start // half * 8
        squares = squares_ref[at : at + 1, start % half : start % half + step]
        inverse = 1.0 / jnp.sqrt(squares / MODEL_WIDTH + EPS)
        inverse = jnp.broadcast_to(inverse, (HEAD_SIZE, step)).T
        inverse_ref[span] = inverse
        pair = mine[span].astype(F32) + other[span].astype(F32)
        key = turn(pair[:, :HEAD_SIZE] * inverse, cos_ref[span], sin_ref[span])
        key_ref[span] = key.astype(BF16)
        value_ref[span] = (pair[:, HEAD_SIZE:] * inverse).astype(BF16)


def attend_rows(turn_of, section, core, operands, piece_ref):
    mine_ref, other_ref, cos_ref, sin_ref, key_ref, value_ref, inverse_ref = operands
    rows = piece_ref.shape[0]
    seq_len = key_ref.shape[0]
    heads = QUERY_COLS // HEAD_SIZE
    scale_by = 1.4426950408889634 / (HEAD_SIZE**0.5)
    span = target_rows(section, core, turn_of, rows)
    first = lax.rem(section + OFFSETS[turn_of] + 4 * core, SECTIONS) * rows
    here = slice(turn_of * rows, (turn_of + 1) * rows)
    total = mine_ref[here].astype(F32) + other_ref[here].astype(F32)
    cosine, sine, inverse = cos_ref[span], sin_ref[span], inverse_ref[span]
    query = jnp.concatenate(
        [
            turn(total[:, h * HEAD_SIZE : (h + 1) * HEAD_SIZE] * inverse, cosine, sine)
            for h in range(heads)
        ],
        axis=0,
    ).astype(BF16)

    def run(count):
        score = lax.dot_general(
            query, key_ref[:count], (((1,), (1,)), ((), ())), preferred_element_type=F32
        )
        row = lax.broadcasted_iota(jnp.int32, (rows, count), 0) + first
        mask = row >= lax.broadcasted_iota(jnp.int32, (rows, count), 1)
        mask = jnp.concatenate([mask] * heads, axis=0)
        score = jnp.where(mask, score, F32(-1e30))
        top = jnp.max(score, axis=1, keepdims=True)
        expo = jnp.exp2((score - top) * scale_by)
        weight_sum = jnp.sum(expo, axis=1, keepdims=True)
        mixed = jnp.dot(expo.astype(BF16), value_ref[:count], preferred_element_type=F32)
        mixed = (mixed / weight_sum).astype(BF16)
        for h in range(heads):
            piece_ref[:, h * HEAD_SIZE : (h + 1) * HEAD_SIZE] = mixed[h * rows : (h + 1) * rows]

    early = first < seq_len // 2
    pl.when(early)(lambda: run(seq_len // 2))
    pl.when(jnp.logical_not(early))(lambda: run(seq_len))
    piece_ref[:, KEY_AT:VALUE_AT] = key_ref[span]
    piece_ref[:, VALUE_AT:] = value_ref[span]


def first_kernel(section_ref, core_ref, *refs):
    mine_ref, other_ref, pair_ref, other_pair_ref, squares_ref, cos_ref, sin_ref = refs[:7]
    piece_ref, *made = refs[7:]
    prepare_keys(pair_ref, other_pair_ref, squares_ref, cos_ref, sin_ref, *made)
    operands = (mine_ref, other_ref, cos_ref, sin_ref, *made)
    attend_rows(0, section_ref[0], core_ref[0], operands, piece_ref)


def next_kernel(turn_of, section_ref, core_ref, *refs):
    attend_rows(turn_of, section_ref[0], core_ref[0], refs[:-1], refs[-1])


def attend(section, core, mine, other, pair, other_pair, squares, cosine, sine):
    seq_len = pair.shape[0]
    piece = jax.ShapeDtypeStruct((seq_len // SECTIONS, WIDE), BF16)
    head = jax.ShapeDtypeStruct((seq_len, HEAD_SIZE), BF16)
    inverse = jax.ShapeDtypeStruct((seq_len, HEAD_SIZE), F32)
    piece_of_first, *made = pl.pallas_call(
        first_kernel,
        in_specs=[scalar()] * 2 + whole(7),
        out_specs=whole(4),
        out_shape=[piece, head, head, inverse],
        compiler_params=params(16),
    )(section, core, mine, other, pair, other_pair, squares, cosine, sine)
    pieces = [piece_of_first]
    for turn_of in range(1, 4):
        pieces.append(
            pl.pallas_call(
                functools.partial(next_kernel, turn_of),
                in_specs=[scalar()] * 2 + whole(7),
                out_specs=pl.BlockSpec(memory_space=VMEM),
                out_shape=piece,
                compiler_params=params(16),
            )(section, core, mine, other, cosine, sine, *made)
        )
    return pieces


def send_rows(pieces):
    arrived = []
    for offset, piece in zip(OFFSETS, pieces):
        pairs = [
            (2 * s + c, 2 * ((s + offset + 4 * c) % SECTIONS) + s // 4)
            for s in range(SECTIONS)
            for c in range(2)
        ]
        arrived.append(lax.ppermute(piece, ("section", "tp"), pairs))
    return arrived


def place_kernel(section_ref, *refs):
    arrived = refs[:4]
    outs, sems = refs[4:7], refs[7]
    copies = []
    for offset, piece in zip(OFFSETS, arrived):
        group = lax.rem(section_ref[0] + SECTIONS - offset, 4)
        for out, start, size in zip(
            outs, (0, KEY_AT, VALUE_AT), (QUERY_COLS, HEAD_SIZE, HEAD_SIZE)
        ):
            at = pl.multiple_of(group * size, HEAD_SIZE)
            copy = pltpu.make_async_copy(
                piece.at[:, start : start + size],
                out.at[0, :, pl.ds(at, size)],
                sems.at[len(copies)],
            )
            copy.start()
            copies.append(copy)
    for copy in copies:
        copy.wait()


def place(section, arrived):
    rows = arrived[0].shape[0]
    return pl.pallas_call(
        place_kernel,
        in_specs=[scalar()] + whole(4, pl.ANY),
        out_specs=whole(3, pl.ANY),
        out_shape=[
            jax.ShapeDtypeStruct((1, rows, 4 * QUERY_COLS), BF16),
            jax.ShapeDtypeStruct((1, rows, 4 * HEAD_SIZE), BF16),
            jax.ShapeDtypeStruct((1, rows, 4 * HEAD_SIZE), BF16),
        ],
        scratch_shapes=[pltpu.SemaphoreType.DMA((12,))],
        compiler_params=params(8),
    )(section, *arrived)


def tables(rows):
    index = jnp.arange(HEAD_SIZE // 2).astype(F32)
    freqs = jnp.exp(index * (-2.0 / HEAD_SIZE) * jnp.log(F32(THETA)))
    angles = jnp.arange(rows).astype(F32)[:, None] * freqs[None, :]
    cosine, sine = jnp.cos(angles), jnp.sin(angles)
    return jnp.concatenate([cosine, cosine], axis=1), jnp.concatenate([-sine, sine], axis=1)


def local(tokens, norm_gain, query_weight, key_weight, value_matrix):
    seq_len = tokens.shape[1]
    section = lax.axis_index("section").astype(jnp.int32).reshape(1)
    core_index = lax.axis_index("tp").astype(jnp.int32)
    core = core_index.reshape(1)

    halves = stripes(core, tokens, norm_gain.reshape(1, -1))
    weight = gather_weights(core, query_weight, key_weight, value_matrix)
    cosine, sine = tables(seq_len)
    (upper, upper_far), (lower, lower_far) = (spread(half) for half in halves)
    near = [block for pair in zip(upper, lower) for block in pair]
    total, sums = near_sum(section, weight, near)
    mine, send, pair, squares = far_sum(
        section, core, weight, total, sums, upper_far + lower_far
    )
    other, other_pair = swap_cores(send), swap_cores(pair)
    pieces = attend(section, core, mine, other, pair, other_pair, squares, cosine, sine)
    return place(section, send_rows(pieces))


def solution(mesh):
    in_specs = (
        P("inst", None, "section"),
        P("section"),
        P(("section", "inst"), "tp"),
        P(("section", "inst"), "tp"),
        P(("section", "inst"), "tp"),
    )
    out_specs = (P("inst", "section", "tp"),) * 3
    return jax.shard_map(local, mesh=mesh, in_specs=in_specs, out_specs=out_specs, check_vma=False)
```

```python
import functools

import jax
import jax.numpy as jnp
from jax import lax
from jax.experimental import pallas as pl
from jax.experimental.pallas import tpu as pltpu
from jax.sharding import PartitionSpec as P

MODEL_WIDTH = 8192
HEAD_SIZE = 128
EPS = 1e-05
THETA = 500000.0
F32 = jnp.float32
BF16 = jnp.bfloat16
VMEM = pltpu.MemorySpace.VMEM
SMEM = pltpu.MemorySpace.SMEM
HBM = pltpu.MemorySpace.HBM
SECTIONS = 8
INSTS = 16
SIDE = 4
STRIPE = 32
EXTRA = 16
QUERY_COLS = 4 * HEAD_SIZE
KEY_AT = QUERY_COLS
VALUE_AT = QUERY_COLS + HEAD_SIZE
WIDE = QUERY_COLS + 2 * HEAD_SIZE


def params(mebibytes):
    return pltpu.CompilerParams(vmem_limit_bytes=mebibytes * 1024 * 1024)


def whole(count, space=VMEM):
    return [pl.BlockSpec(memory_space=space)] * count


def scalar():
    return pl.BlockSpec(memory_space=SMEM)


def z_shift(array, step):
    return lax.ppermute(array, "section", [(i, (i + step) % SECTIONS) for i in range(SECTIONS)])


def xy_shift(array, dx, dy):
    pairs = [
        (x * SIDE + y, ((x + dx) % SIDE) * SIDE + (y + dy) % SIDE)
        for x in range(SIDE)
        for y in range(SIDE)
    ]
    return lax.ppermute(array, "inst", pairs)


def gather_square(shard, first, second):
    line = [shard] + [xy_shift(shard, -step * first[0], -step * first[1]) for step in range(1, SIDE)]
    line = jnp.stack(line)
    before, behind = xy_shift(line, *second), xy_shift(line, -second[0], -second[1])
    return [line, behind, xy_shift(before, *second), before]


def swap_cores(array):
    return lax.ppermute(array, "tp", [(0, 1), (1, 0)])


def stripe_kernel(core_ref, square_ref, token_ref, gain_ref, out_ref):
    width, half = token_ref.shape[2], out_ref.shape[1]
    rows = token_ref.shape[1] // 2
    feature = lax.broadcasted_iota(jnp.int32, (width, half), 0)
    lane = lax.broadcasted_iota(jnp.int32, (width, half), 1)
    inst = lane // STRIPE
    x = (inst // SIDE + square_ref[0]) % SIDE
    y = (inst % SIDE + square_ref[1]) % SIDE
    wanted = (x * SIDE + y) * (2 * STRIPE) + core_ref[0] * STRIPE + lane % STRIPE
    pick = jnp.where(feature == wanted, 1.0, 0.0).astype(BF16)
    extra = jnp.zeros((EXTRA, rows), BF16)
    row = lax.broadcasted_iota(jnp.int32, extra.shape, 0)
    for index in range(2):
        span = slice(index * rows, (index + 1) * rows)
        floats = token_ref[0, span].astype(F32)
        scaled = (floats * gain_ref[...]).astype(BF16)
        out_ref[span] = jnp.dot(scaled, pick, preferred_element_type=F32).astype(BF16)
        squares = jnp.sum(floats * floats, axis=1, keepdims=True)
        squares = jnp.broadcast_to(squares, (rows, HEAD_SIZE)).T[:EXTRA]
        high = squares.astype(BF16)
        low = (squares - high.astype(F32)).astype(BF16)
        extra = jnp.where(row == 2 * index, high, jnp.where(row == 2 * index + 1, low, extra))
    out_ref[2 * rows :] = extra


def stripes(core, square, tokens, gain):
    _, seq_len, width = tokens.shape
    shape = jax.ShapeDtypeStruct((seq_len + EXTRA, width // 2), BF16)
    return pl.pallas_call(
        stripe_kernel,
        in_specs=[scalar()] * 2 + whole(2),
        out_specs=pl.BlockSpec(memory_space=VMEM),
        out_shape=shape,
        compiler_params=params(20),
    )(core, square, tokens, gain)


def cut_far_kernel(before_ref, behind_ref, left_ref, right_ref):
    half = left_ref.shape[1]
    left_ref[...] = before_ref[:, :half]
    right_ref[...] = behind_ref[:, half:]


def cut_far(before, behind):
    rows, cols = before.shape
    shape = jax.ShapeDtypeStruct((rows, cols // 2), BF16)
    return pl.pallas_call(
        cut_far_kernel,
        in_specs=whole(2),
        out_specs=whole(2),
        out_shape=[shape, shape],
        cost_estimate=pl.CostEstimate(flops=1_000_000_000, transcendentals=0, bytes_accessed=2_000_000),
        compiler_params=params(8),
    )(before, behind)


def spread(block):
    blocks = [block] * SECTIONS
    before, behind = block, block
    for step in range(1, 4):
        before, behind = z_shift(before, 1), z_shift(behind, -1)
        blocks[SECTIONS - step], blocks[step] = before, behind
    left, right = cut_far(before, behind)
    return [blocks[d] for d in NEAR], [z_shift(left, 1), z_shift(right, -1)]


def cut_kernel(core_ref, query_ref, key_ref, value_ref, keep_ref, send_ref):
    core = core_ref[0]
    for ref, first in ((keep_ref, core), (send_ref, 1 - core)):
        rows = pl.ds(pl.multiple_of(first * STRIPE, STRIPE), STRIPE)
        start = 0
        for source in (query_ref, key_ref, value_ref):
            ref[:, start : start + source.shape[1]] = source[rows, :]
            start += source.shape[1]


def sort_kernel(core_ref, keep_ref, other_ref, out_ref):
    first = core_ref[0] == 0
    keep, other = keep_ref[...], other_ref[...]
    groups = out_ref.shape[0] // 2
    for side in range(2):
        mine = first if side == 0 else jnp.logical_not(first)
        columns = jnp.where(mine, keep, other)
        for group in range(groups):
            start = 0
            for size, at in ((QUERY_COLS, 0), (HEAD_SIZE, KEY_AT), (HEAD_SIZE, VALUE_AT)):
                out_ref[side * groups + group, :, at : at + size] = columns[
                    :, start + group * size : start + (group + 1) * size
                ]
                start += groups * size


def gather_weights(core, query_weight, key_weight, value_matrix):
    cols = query_weight.shape[1] + key_weight.shape[1] + value_matrix.shape[1]
    shape = jax.ShapeDtypeStruct((STRIPE, cols), BF16)
    keep, send = pl.pallas_call(
        cut_kernel,
        in_specs=[scalar()] + whole(3),
        out_specs=whole(2),
        out_shape=[shape, shape],
        compiler_params=params(8),
    )(core, query_weight, key_weight, value_matrix)
    blocks = pl.pallas_call(
        sort_kernel,
        in_specs=[scalar()] + whole(2),
        out_specs=pl.BlockSpec(memory_space=VMEM),
        out_shape=jax.ShapeDtypeStruct((SECTIONS, STRIPE, WIDE), BF16),
        compiler_params=params(8),
    )(core, keep, swap_cores(send))
    blocks = lax.all_to_all(blocks, "section", 0, 0, tiled=True)
    half = WIDE // 2
    left = gather_square(blocks[..., :half], (0, 1), (1, 0))
    right = gather_square(blocks[..., half:], (1, 0), (0, 1))
    return left + right


def load_weights(weight_hbm, source, target, sems):
    half = WIDE // 2
    copies = []
    for far in range(SIDE):
        for lines, place in (
            (weight_hbm[:SIDE], target.at[far, :, :, :half]),
            (weight_hbm[SIDE:], target.at[:, far, :, half:]),
        ):
            copies.append(
                pltpu.make_async_copy(lines[far].at[:, source], place, sems.at[len(copies)])
            )
    return copies


NEAR = (0, 1, 7, 2, 6, 3, 5)


def add_squares(squares, extra, half):
    extra = extra.astype(F32)
    return squares + extra[2 * half : 2 * half + 1] + extra[2 * half + 1 : 2 * half + 2]


def near_kernel(section_ref, *refs):
    weight_hbm, block_hbm = refs[: 2 * SIDE], refs[2 * SIDE : -7]
    total_ref, squares_ref, weight, blocks, total, weight_sems, block_sems = refs[-7:]
    loads = []
    for place, distance in enumerate(NEAR):
        source = lax.rem(section_ref[0] + distance, SECTIONS)
        load = load_weights(weight_hbm, source, weight.at[place], weight_sems.at[place])
        load.append(
            pltpu.make_async_copy(block_hbm[place], blocks.at[place], block_sems.at[place])
        )
        loads.append(load)
    ahead = 2
    for load in loads[:ahead]:
        for copy in load:
            copy.start()
    rows = total_ref.shape[0] // 2
    width = block_hbm[0].shape[1]
    squares = [jnp.zeros((1, width), F32)] * 2
    for place in range(len(NEAR)):
        for copy in loads[place]:
            copy.wait()
        if place + ahead < len(NEAR):
            for copy in loads[place + ahead]:
                copy.start()
        matrix = weight[place].reshape(INSTS * STRIPE, WIDE)
        for half in range(2):
            span = slice(half * rows, (half + 1) * rows)
            block = blocks.at[place]
            part = jnp.dot(block[span], matrix, preferred_element_type=F32)
            squares[half] = add_squares(squares[half], block[2 * rows :], half)
            if place == 0:
                total[span] = part
            elif place + 1 < len(NEAR):
                total[span] += part
            else:
                total_ref[span] = (part + total[span]).astype(BF16)
    for half in range(2):
        squares_ref[half * 8 : (half + 1) * 8] = jnp.broadcast_to(squares[half], (8, width))


def near_sum(section, weight, blocks):
    rows, width = blocks[0].shape
    seq_len = rows - EXTRA
    return pl.pallas_call(
        near_kernel,
        in_specs=[scalar()] + whole(len(weight) + len(blocks), HBM),
        out_specs=whole(2),
        out_shape=[
            jax.ShapeDtypeStruct((seq_len, WIDE), BF16),
            jax.ShapeDtypeStruct((16, width), F32),
        ],
        scratch_shapes=[
            pltpu.VMEM((len(NEAR), SIDE, SIDE, STRIPE, WIDE), BF16),
            pltpu.VMEM((len(blocks), *blocks[0].shape), BF16),
            pltpu.VMEM((seq_len, WIDE), F32),
            pltpu.SemaphoreType.DMA((len(NEAR), 2 * SIDE)),
            pltpu.SemaphoreType.DMA((len(blocks),)),
        ],
        compiler_params=params(60),
    )(section, *weight, *blocks)


OFFSETS = (0, 5, 2, 7)


def target_rows(section, core, turn_of, rows):
    target = lax.rem(section + OFFSETS[turn_of] + 4 * core, SECTIONS)
    return pl.ds(pl.multiple_of(target * rows, rows), rows)


def far_kernel(section_ref, core_ref, total_hbm, sums_ref, *refs):
    weight_hbm, block_hbm = refs[: 2 * SIDE], refs[2 * SIDE : -12]
    mine_hbm, send_hbm, pair_hbm, squares_ref = refs[-12:-8]
    weight, total, blocks, out, weight_sems, sems, block_sems, out_sems = refs[-8:]
    rows = total.shape[1]
    source = lax.rem(section_ref[0] + SECTIONS // 2, SECTIONS)
    weight_loads = load_weights(weight_hbm, source, weight, weight_sems)
    for copy in weight_loads:
        copy.start()
    loads = []
    for half in range(2):
        span = slice(half * rows, (half + 1) * rows)
        group = [pltpu.make_async_copy(total_hbm.at[span], total.at[half], sems.at[half])]
        if half == 0:
            for index in range(2):
                group.append(
                    pltpu.make_async_copy(block_hbm[index], blocks.at[index], block_sems.at[index])
                )
        for copy in group:
            copy.start()
        loads.append(group)
    for copy in weight_loads:
        copy.wait()
    matrix = weight[...].reshape(INSTS * STRIPE, WIDE)
    stores = []
    for half in range(2):
        span = slice(half * rows, (half + 1) * rows)
        for copy in loads[half]:
            copy.wait()
        block = jnp.concatenate([blocks[0, span], blocks[1, span]], axis=1)
        part = jnp.dot(block, matrix, preferred_element_type=F32)
        out[span] = (part + total[half].astype(F32)).astype(BF16)
        at = slice(half * 8, (half + 1) * 8)
        extra = jnp.concatenate([blocks[0, 2 * rows :], blocks[1, 2 * rows :]], axis=1)
        squares_ref[at] = add_squares(sums_ref[at], extra, half)
        store = pltpu.make_async_copy(
            out.at[span, QUERY_COLS:], pair_hbm.at[span], out_sems.at[half]
        )
        store.start()
        stores.append(store)
    chunk = 2 * rows // SECTIONS
    for core, target in ((1 - core_ref[0], send_hbm), (core_ref[0], mine_hbm)):
        for turn_of in range(4):
            store = pltpu.make_async_copy(
                out.at[target_rows(section_ref[0], core, turn_of, chunk), :QUERY_COLS],
                target.at[turn_of * chunk : (turn_of + 1) * chunk],
                out_sems.at[len(stores)],
            )
            store.start()
            stores.append(store)
    for store in stores:
        store.wait()


def far_sum(section, core, weight, total, sums, blocks):
    seq_len = total.shape[0]
    rows = seq_len // 2
    queries = jax.ShapeDtypeStruct((rows, QUERY_COLS), BF16)
    return pl.pallas_call(
        far_kernel,
        in_specs=[scalar()] * 2
        + whole(1, HBM)
        + whole(1)
        + whole(len(weight) + len(blocks), HBM),
        out_specs=whole(3, HBM) + whole(1),
        out_shape=[
            queries,
            queries,
            jax.ShapeDtypeStruct((seq_len, WIDE - QUERY_COLS), BF16),
            jax.ShapeDtypeStruct(sums.shape, F32),
        ],
        scratch_shapes=[
            pltpu.VMEM((SIDE, SIDE, STRIPE, WIDE), BF16),
            pltpu.VMEM((2, rows, WIDE), BF16),
            pltpu.VMEM((2, *blocks[0].shape), BF16),
            pltpu.VMEM((seq_len, WIDE), BF16),
            pltpu.SemaphoreType.DMA((2 * SIDE,)),
            pltpu.SemaphoreType.DMA((2,)),
            pltpu.SemaphoreType.DMA((2,)),
            pltpu.SemaphoreType.DMA((10,)),
        ],
        compiler_params=params(60),
    )(section, core, total, sums, *weight, *blocks)


def turn(head, cosine, sine):
    return head * cosine + pltpu.roll(head, HEAD_SIZE // 2, 1) * sine


def prepare_keys(mine, other, squares_ref, cos_ref, sin_ref, key_ref, value_ref, inverse_ref):
    step = 256
    half = squares_ref.shape[1]
    for start in range(0, key_ref.shape[0], step):
        span = slice(start, start + step)
        at = start // half * 8
        squares = squares_ref[at : at + 1, start % half : start % half + step]
        inverse = 1.0 / jnp.sqrt(squares / MODEL_WIDTH + EPS)
        inverse = jnp.broadcast_to(inverse, (HEAD_SIZE, step)).T
        inverse_ref[span] = inverse
        pair = mine[span].astype(F32) + other[span].astype(F32)
        key = turn(pair[:, :HEAD_SIZE] * inverse, cos_ref[span], sin_ref[span])
        key_ref[span] = key.astype(BF16)
        value_ref[span] = (pair[:, HEAD_SIZE:] * inverse).astype(BF16)


def attend_rows(turn_of, section, core, operands, piece_ref):
    mine_ref, other_ref, cos_ref, sin_ref, key_ref, value_ref, inverse_ref = operands
    rows = piece_ref.shape[0]
    seq_len = key_ref.shape[0]
    heads = QUERY_COLS // HEAD_SIZE
    scale_by = 1.4426950408889634 / (HEAD_SIZE**0.5)
    span = target_rows(section, core, turn_of, rows)
    first = lax.rem(section + OFFSETS[turn_of] + 4 * core, SECTIONS) * rows
    here = slice(turn_of * rows, (turn_of + 1) * rows)
    total = mine_ref[here].astype(F32) + other_ref[here].astype(F32)
    cosine, sine, inverse = cos_ref[span], sin_ref[span], inverse_ref[span]
    query = jnp.concatenate(
        [
            turn(total[:, h * HEAD_SIZE : (h + 1) * HEAD_SIZE] * inverse, cosine, sine)
            for h in range(heads)
        ],
        axis=0,
    ).astype(BF16)

    def run(count):
        score = lax.dot_general(
            query, key_ref[:count], (((1,), (1,)), ((), ())), preferred_element_type=F32
        )
        row = lax.broadcasted_iota(jnp.int32, (rows, count), 0) + first
        mask = row >= lax.broadcasted_iota(jnp.int32, (rows, count), 1)
        mask = jnp.concatenate([mask] * heads, axis=0)
        score = jnp.where(mask, score, F32(-1e30))
        top = jnp.max(score, axis=1, keepdims=True)
        expo = jnp.exp2((score - top) * scale_by)
        weight_sum = jnp.sum(expo, axis=1, keepdims=True)
        mixed = jnp.dot(expo.astype(BF16), value_ref[:count], preferred_element_type=F32)
        mixed = (mixed / weight_sum).astype(BF16)
        for h in range(heads):
            piece_ref[:, h * HEAD_SIZE : (h + 1) * HEAD_SIZE] = mixed[h * rows : (h + 1) * rows]

    early = first < seq_len // 2
    pl.when(early)(lambda: run(seq_len // 2))
    pl.when(jnp.logical_not(early))(lambda: run(seq_len))
    piece_ref[:, KEY_AT:VALUE_AT] = key_ref[span]
    piece_ref[:, VALUE_AT:] = value_ref[span]


def first_kernel(section_ref, core_ref, *refs):
    mine_ref, other_ref, pair_ref, other_pair_ref, squares_ref, cos_ref, sin_ref = refs[:7]
    piece_ref, *made = refs[7:]
    prepare_keys(pair_ref, other_pair_ref, squares_ref, cos_ref, sin_ref, *made)
    operands = (mine_ref, other_ref, cos_ref, sin_ref, *made)
    attend_rows(0, section_ref[0], core_ref[0], operands, piece_ref)


def next_kernel(turn_of, section_ref, core_ref, *refs):
    attend_rows(turn_of, section_ref[0], core_ref[0], refs[:-1], refs[-1])


def attend(section, core, mine, other, pair, other_pair, squares, cosine, sine):
    seq_len = pair.shape[0]
    piece = jax.ShapeDtypeStruct((seq_len // SECTIONS, WIDE), BF16)
    head = jax.ShapeDtypeStruct((seq_len, HEAD_SIZE), BF16)
    inverse = jax.ShapeDtypeStruct((seq_len, HEAD_SIZE), F32)
    piece_of_first, *made = pl.pallas_call(
        first_kernel,
        in_specs=[scalar()] * 2 + whole(7),
        out_specs=whole(4),
        out_shape=[piece, head, head, inverse],
        compiler_params=params(16),
    )(section, core, mine, other, pair, other_pair, squares, cosine, sine)
    pieces = [piece_of_first]
    for turn_of in range(1, 4):
        pieces.append(
            pl.pallas_call(
                functools.partial(next_kernel, turn_of),
                in_specs=[scalar()] * 2 + whole(7),
                out_specs=pl.BlockSpec(memory_space=VMEM),
                out_shape=piece,
                compiler_params=params(16),
            )(section, core, mine, other, cosine, sine, *made)
        )
    return pieces


def send_rows(pieces):
    arrived = []
    for offset, piece in zip(OFFSETS, pieces):
        pairs = [
            (2 * s + c, 2 * ((s + offset + 4 * c) % SECTIONS) + s // 4)
            for s in range(SECTIONS)
            for c in range(2)
        ]
        arrived.append(lax.ppermute(piece, ("section", "tp"), pairs))
    return arrived


def place_kernel(section_ref, *refs):
    arrived = refs[:4]
    outs, sems = refs[4:7], refs[7]
    copies = []
    for offset, piece in zip(OFFSETS, arrived):
        group = lax.rem(section_ref[0] + SECTIONS - offset, 4)
        for out, start, size in zip(
            outs, (0, KEY_AT, VALUE_AT), (QUERY_COLS, HEAD_SIZE, HEAD_SIZE)
        ):
            at = pl.multiple_of(group * size, HEAD_SIZE)
            copy = pltpu.make_async_copy(
                piece.at[:, start : start + size],
                out.at[0, :, pl.ds(at, size)],
                sems.at[len(copies)],
            )
            copy.start()
            copies.append(copy)
    for copy in copies:
        copy.wait()


def place(section, arrived):
    rows = arrived[0].shape[0]
    return pl.pallas_call(
        place_kernel,
        in_specs=[scalar()] + whole(4, pl.ANY),
        out_specs=whole(3, pl.ANY),
        out_shape=[
            jax.ShapeDtypeStruct((1, rows, 4 * QUERY_COLS), BF16),
            jax.ShapeDtypeStruct((1, rows, 4 * HEAD_SIZE), BF16),
            jax.ShapeDtypeStruct((1, rows, 4 * HEAD_SIZE), BF16),
        ],
        scratch_shapes=[pltpu.SemaphoreType.DMA((12,))],
        compiler_params=params(8),
    )(section, *arrived)


def tables(rows):
    index = jnp.arange(HEAD_SIZE // 2).astype(F32)
    freqs = jnp.exp(index * (-2.0 / HEAD_SIZE) * jnp.log(F32(THETA)))
    angles = jnp.arange(rows).astype(F32)[:, None] * freqs[None, :]
    cosine, sine = jnp.cos(angles), jnp.sin(angles)
    return jnp.concatenate([cosine, cosine], axis=1), jnp.concatenate([-sine, sine], axis=1)


def local(tokens, norm_gain, query_weight, key_weight, value_matrix):
    seq_len = tokens.shape[1]
    section = lax.axis_index("section").astype(jnp.int32).reshape(1)
    core_index = lax.axis_index("tp").astype(jnp.int32)
    core = core_index.reshape(1)

    inst = lax.axis_index("inst").astype(jnp.int32)
    square = jnp.stack([inst // SIDE, inst % SIDE])
    block = stripes(core, square, tokens, norm_gain.reshape(1, -1))
    weight = gather_weights(core, query_weight, key_weight, value_matrix)
    cosine, sine = tables(seq_len)
    near, far = spread(block)
    total, sums = near_sum(section, weight, near)
    mine, send, pair, squares = far_sum(
        section, core, weight, total, sums, far
    )
    other, other_pair = swap_cores(send), swap_cores(pair)
    pieces = attend(section, core, mine, other, pair, other_pair, squares, cosine, sine)
    return place(section, send_rows(pieces))


def solution(mesh):
    in_specs = (
        P("inst", None, "section"),
        P("section"),
        P(("section", "inst"), "tp"),
        P(("section", "inst"), "tp"),
        P(("section", "inst"), "tp"),
    )
    out_specs = (P("inst", "section", "tp"),) * 3
    return jax.shard_map(local, mesh=mesh, in_specs=in_specs, out_specs=out_specs, check_vma=False)
```
